512 devices in a mesh: blk: 16 (over z_lo, y), group: 32 (over z_hi, x, core).
Axes of the slice: x: 4, y: 8, z: 8 (z_hi: 4, z_lo: 2; z = z_hi * 2 + z_lo), core: 2. Of those that a mesh axis runs over, the one named last changes fastest.
Arguments:
- audio: bfloat16 [81920, 1024], P(('blk', 'group')), may hold values from -3 to 3
- text: bfloat16 [81920, 768], P(('blk', 'group')), may hold values from -4 to 4
- labels: int32 [81920], P(('blk', 'group')), may hold values from 0 to 319
- audio_weight: bfloat16 [1024, 768], P('group'), may hold values from -0.1875 to 0.1875
Outputs:
- audio_grad: bfloat16 [81920, 1024], P(('blk', 'group'))
- text_grad: bfloat16 [81920, 768], P(('blk', 'group'))
- weight_grad: float32 [1024, 768], P('group')
The draws below stay inside these ranges and needn't reach their ends.
All inputs are finite; a program needn't handle non-finite values.
Results may differ from the reference program's by a relative error of at most 0.024.
Values may be sent and summed in bfloat16 or wider, within the bound.
A program may use at most 64 MiB of HBM per device.

```python
import math
import jax
import jax.numpy as jnp
from jax import lax

D = 1024
P_SIZE = 768
ROWS_DEV = 160
B = 81920
SPEAKERS = 320
N_BLK = 16
N_GROUP = 32


def draw_text(key, part):
    key = jax.random.fold_in(key, 11)
    key_rows, key_cols, key_base = jax.random.split(key, 3)
    rows = jnp.exp(jax.random.uniform(key_rows, (B, 1), minval=math.log(0.05), maxval=math.log(0.5)))
    cols = jnp.exp(jax.random.uniform(key_cols, (1, P_SIZE), minval=math.log(0.5), maxval=math.log(2.0)))
    base = jax.random.truncated_normal(key_base, -4.0, 4.0, (B, P_SIZE))
    return (base * rows * cols).astype(jnp.bfloat16)


def with_ends(result, rng, low, largest):
    index_at = [jax.random.randint(jax.random.fold_in(rng, axis), (), 0, length) for axis, length in enumerate(result.shape)]
    widest = result.shape.index(max(result.shape))
    neighbour = index_at[:widest] + [(index_at[widest] + 1) % result.shape[widest]] + index_at[widest + 1:]
    return result.at[tuple(index_at)].set(low).at[tuple(neighbour)].set(largest)


def with_spikes(drawn, rng, source, target, parts, factor):
    owner, partner = [(jnp.arange(drawn.shape[axis_at]) // (drawn.shape[axis_at] // parts)).reshape([-1 if axis == axis_at else 1 for axis in range(drawn.ndim)]) for axis_at in (source, target)]
    chosen = jax.random.permutation(rng, parts)[partner]
    strong = (owner == chosen) | (owner == (partner + parts // 2) % parts)
    return jnp.where(strong, factor * drawn, drawn)


def levels(own_key, shape, cuts, low, top_value):
    def one(position, blocks):
        heights = jax.random.uniform(jax.random.fold_in(jax.random.fold_in(own_key, 6), position), (blocks,), jnp.float32, low / len(cuts), top_value / len(cuts))
        return jnp.repeat(jnp.exp(heights), shape[position] // blocks).reshape((-1,) + (1,) * (len(shape) - position - 1))

    level = one(*cuts[0])
    for cut in cuts[1:]:
        level = level * one(*cut)
    return level


def normal_values(own_key, dims, scale, limit, cuts=(), dtype=jnp.bfloat16):
    array = scale * jax.random.normal(own_key, dims, jnp.float32)
    if cuts:
        array = array * levels(own_key, dims, cuts, -0.22, 0.18)
    return jnp.clip(array, -limit, limit).astype(dtype)


def heavy_noise(own_key, extent, deviation, most, pieces, heavy, dtype=jnp.bfloat16):
    entries = deviation * jax.random.normal(own_key, extent, jnp.float32)
    if pieces:
        entries = entries * levels(own_key, extent, pieces, -0.22, 0.18)
    return jnp.clip(with_spikes(entries, jax.random.fold_in(own_key, 3), *heavy), -most, most).astype(dtype)


def setup_inputs(seed: int = 0) -> dict:
    key_of = jax.random.split(jax.random.key(seed), 5)
    audio = heavy_noise(key_of[0], (B, D), 0.05, 3.0, ((0, 512),), (0, 1, 512, 6.0))
    text = draw_text(jax.random.fold_in(key_of[4], 71), 0)
    labels = with_ends(jax.random.randint(key_of[2], (B,), 0, SPEAKERS), jax.random.fold_in(key_of[2], 1), 0, SPEAKERS - 1).astype(jnp.int32)
    audio_weight = normal_values(key_of[3], (D, P_SIZE), D ** -0.5, 0.1875, ((0, 32),))
    return {"audio": audio, "text": text, "labels": labels, "audio_weight": audio_weight}


SCALE = 16.0
SHIFT = -4.0

def unit_rows(values):
    norm = jnp.sqrt(lax.optimization_barrier(jnp.sum(values * values, axis=-1, keepdims=True)) + 1e-06)
    return (values / norm, norm)

def regroup(values):
    width = values.shape[-1]
    return values.reshape(N_BLK, N_GROUP, ROWS_DEV, width).transpose(1, 0, 2, 3).reshape(N_GROUP, N_BLK * ROWS_DEV, width)

def ungroup(values):
    width = values.shape[-1]
    return values.reshape(N_GROUP, N_BLK, ROWS_DEV, width).transpose(1, 0, 2, 3).reshape(B, width)

def set_terms(item):
    audio_set, text_set, label_set = item
    logits = SCALE * jnp.dot(audio_set, text_set.T, preferred_element_type=jnp.float32) + SHIFT
    positive = (label_set[:, None] == label_set[None, :]).astype(jnp.float32)
    weights = (SCALE * (jax.nn.sigmoid(logits) - positive)).astype(jnp.bfloat16).astype(jnp.float32)
    d_audio = jnp.dot(weights, text_set, preferred_element_type=jnp.float32)
    d_text = jnp.dot(weights.T, audio_set, preferred_element_type=jnp.float32)
    return (d_audio, d_text)

def reference(audio, text, labels, audio_weight):
    proj = jnp.dot(audio, audio_weight, preferred_element_type=jnp.float32)
    unit_a, norm_a = unit_rows(proj)
    audio_unit = unit_a.astype(jnp.bfloat16)
    unit_t, norm_t = unit_rows(text.astype(jnp.float32))
    text_unit = unit_t.astype(jnp.bfloat16)
    audio_sets = regroup(audio_unit.astype(jnp.float32))
    text_sets = regroup(text_unit.astype(jnp.float32))
    label_sets = regroup(labels.reshape(B, 1))[:, :, 0]
    d_audio, d_text = lax.map(set_terms, (audio_sets, text_sets, label_sets))
    d_audio = ungroup(d_audio)
    d_text = ungroup(d_text)
    dproj = (d_audio - unit_a * lax.optimization_barrier(jnp.sum(unit_a * d_audio, axis=-1, keepdims=True))) / norm_a
    dproj_low = dproj.astype(jnp.bfloat16)
    audio_grad = jnp.dot(dproj_low, audio_weight.T, preferred_element_type=jnp.float32).astype(jnp.bfloat16)
    text_grad = ((d_text - unit_t * lax.optimization_barrier(jnp.sum(unit_t * d_text, axis=-1, keepdims=True))) / norm_t).astype(jnp.bfloat16)
    count = N_BLK * N_GROUP
    audio_pieces = audio.reshape(count, ROWS_DEV, D)
    dproj_pieces = dproj_low.reshape(count, ROWS_DEV, P_SIZE)

    def add_piece(total, pair):
        part = jnp.dot(pair[0].T, pair[1], preferred_element_type=jnp.float32)
        part = lax.optimization_barrier(part.astype(jnp.bfloat16))
        return (total + part.astype(jnp.float32), None)
    weight_grad, _ = lax.scan(add_piece, jnp.zeros((D, P_SIZE), jnp.float32), (audio_pieces, dproj_pieces))
    return (audio_grad, text_grad, weight_grad)
```

```python
import jax
import jax.numpy as jnp
from jax import lax
from jax.experimental import pallas as pl
from jax.experimental.pallas import tpu as pltpu
from jax.sharding import PartitionSpec as P

MESH = pl.DeviceIdType.MESH
BF = jnp.bfloat16
F32 = jnp.float32
SCALE = 16.0
SHIFT = -4.0
EPS = 1e-6
ROWS, WIDE, COLS, HALF = 160, 1024, 768, 80


def kernel(
    audio_hbm, text_hbm, labels_ref, weight_hbm,
    audio_out, text_out, grad_out,
    audio, text, texts, label_rows, pair_label, weight, units, unit_low, norms, d_audio, d_text,
    dp_low, pair_dp, rs_out, rs_in, audio_res, text_res, grad_res,
    load_sem, store_sem, gs, gr, ls, lr, w1s, w1r, w2s, w2r, wcs, wcr, ps, pr, rss, rsr,
):
    blk, group = lax.axis_index("blk"), lax.axis_index("group")
    z_lo, y = blk // 8, blk % 8
    z_hi, x, core = group // 8, (group // 2) % 4, group % 2

    def at_y(step):
        return (z_lo * 8 + (y + step + 8) % 8, group)

    def at_x(step):
        return (blk, z_hi * 8 + ((x + step) % 4) * 2 + core)

    def at_z(step):
        return (blk, ((z_hi + step) % 4) * 8 + x * 2 + core)

    pair = ((1 - z_lo) * 8 + y, group)
    other = (blk, z_hi * 8 + x * 2 + (1 - core))
    ring = (at_y(1), at_y(-1))
    started = []

    def send(src, dst, s, r, to):
        copy = pltpu.make_async_remote_copy(
            src_ref=src, dst_ref=dst, send_sem=s, recv_sem=r, device_id=to, device_id_type=MESH
        )
        copy.start()
        started.append(copy)

    def arrived(dst, s, r):
        pltpu.make_async_remote_copy(
            src_ref=dst, dst_ref=dst, send_sem=s, recv_sem=r, device_id=ring[0], device_id_type=MESH
        ).wait_recv()

    loads = [
        pltpu.make_async_copy(text_hbm, text, load_sem.at[0]),
        pltpu.make_async_copy(weight_hbm, weight.at[z_hi, x * 2 + core], load_sem.at[1]),
        pltpu.make_async_copy(audio_hbm, audio.at[0], load_sem.at[2]),
    ]
    for load in loads:
        load.start()

    barrier = pltpu.get_barrier_semaphore()
    friends = ring + (pair, other) + tuple(at_z(i) for i in (1, 2, 3)) + tuple(at_x(i) for i in (1, 2, 3))
    for friend in friends:
        pl.semaphore_signal(barrier, inc=1, device_id=friend, device_id_type=MESH)

    loads[0].wait()
    raw = text[...].astype(F32)
    texts[0] = (raw / jnp.sqrt(jnp.sum(raw * raw, axis=-1, keepdims=True) + EPS)).astype(BF)
    label_rows[0] = jnp.broadcast_to(labels_ref[...].astype(F32), (8, ROWS))
    loads[1].wait()
    loads[2].wait()
    pl.semaphore_wait(barrier, len(friends))

    def part(k):
        return pl.ds(k * HALF, HALF)

    def slot_of(d, hop):
        return 2 * hop - 1 + d if hop < 4 else 7

    def gather_send(d, hop, k):
        src = 0 if hop == 1 else slot_of(d, hop - 1)
        send(
            texts.at[src, part(k)], texts.at[slot_of(d, hop), part(k)],
            gs.at[d, hop - 1, k], gr.at[d, hop - 1, k], ring[d],
        )

    def gather_wait(d, hop, k):
        arrived(texts.at[slot_of(d, hop), part(k)], gs.at[d, hop - 1, k], gr.at[d, hop - 1, k])

    def label_send(d, hop):
        src = 0 if hop == 1 else slot_of(d, hop - 1)
        send(
            label_rows.at[src], label_rows.at[slot_of(d, hop)],
            ls.at[d, hop - 1], lr.at[d, hop - 1], ring[d],
        )

    for k in (0, 1):
        for d in (0, 1):
            gather_send(d, 1, d if k == 0 else 1 - d)
    for d in (0, 1):
        label_send(d, 1)
    mine = weight.at[z_hi, x * 2 + core]
    for i in (1, 2, 3):
        send(mine, mine, w1s.at[i - 1], w1r.at[i - 1], at_z(i))
    send(label_rows.at[0], pair_label, ps.at[0], pr.at[0], pair)
    send(audio.at[0], audio.at[1], ps.at[1], pr.at[1], pair)

    def gather_hop(hop):
        for k in (0, 1):
            for d in (0, 1):
                which = d if k == 0 else 1 - d
                if hop == 4 and which != d:
                    continue
                gather_wait(d, hop, which)
                if hop < 3 or (hop == 3 and which == d):
                    gather_send(d, hop + 1, which)
        for d in (0, 1):
            if hop == 4 and d == 1:
                continue
            arrived(label_rows.at[slot_of(d, hop)], ls.at[d, hop - 1], lr.at[d, hop - 1])
            if hop < 3 or (hop == 3 and d == 0):
                label_send(d, hop + 1)

    gather_hop(1)
    for i in (1, 2, 3):
        there = weight.at[(z_hi + 4 - i) % 4, x * 2 + core]
        arrived(there, w1s.at[i - 1], w1r.at[i - 1])
    column = weight.at[:, x * 2 + core]
    for i in (1, 3, 2):
        send(column, column, w2s.at[i - 1], w2r.at[i - 1], at_x(i))
    send(column, column, wcs.at[0], wcr.at[0], other)
    gather_hop(2)
    for i in (1, 3, 2):
        there = weight.at[:, ((x + 4 - i) % 4) * 2 + core]
        arrived(there, w2s.at[i - 1], w2r.at[i - 1])
        send(there, there, wcs.at[i], wcr.at[i], other)
    gather_hop(3)
    for i in range(4):
        there = weight.at[:, ((x + 4 - i) % 4) * 2 + (1 - core)]
        arrived(there, wcs.at[i], wcr.at[i])
    arrived(pair_label, ps.at[0], pr.at[0])
    arrived(audio.at[1], ps.at[1], pr.at[1])

    whole = weight[...].reshape(WIDE, COLS)
    for i in (0, 1):
        proj = jnp.dot(audio[i], whole, preferred_element_type=F32)
        norm = jnp.sqrt(jnp.sum(proj * proj, axis=-1, keepdims=True) + EPS)
        unit = proj / norm
        units[i] = unit
        norms[i] = jnp.broadcast_to(norm, (ROWS, 128))
        unit_low[pl.ds(i * ROWS, ROWS)] = unit.astype(BF)

    diagonal = lax.broadcasted_iota(jnp.int32, (ROWS, ROWS), 0) == lax.broadcasted_iota(
        jnp.int32, (ROWS, ROWS), 1
    )

    def upright(row):
        return jnp.sum(jnp.where(diagonal, row, 0.0), axis=1, keepdims=True)

    own_labels = jnp.concatenate(
        [upright(label_rows[0][0:1, :]), upright(pair_label[...][0:1, :])], axis=0
    )

    d_audio[...] = jnp.zeros_like(d_audio)

    def block(slot):
        rows = texts[slot]
        logits = SCALE * lax.dot_general(
            unit_low[...], rows, (((1,), (1,)), ((), ())), preferred_element_type=F32
        ) + SHIFT
        positive = (own_labels == label_rows[slot][0:1, :]).astype(F32)
        pairs = (SCALE * (jax.nn.sigmoid(logits) - positive)).astype(BF)
        d_audio[...] += jnp.dot(pairs, rows, preferred_element_type=F32)
        d_text[slot] = lax.dot_general(
            pairs, unit_low[...], (((0,), (0,)), ((), ())), preferred_element_type=F32
        )

    def body(slot, carry):
        block(slot)
        return carry

    lax.fori_loop(0, 7, body, 0)

    def rs_send(d, r, k):
        slot = 7 if r == 4 else (2 * r if d == 0 else 2 * r - 1)
        value = d_text[slot, part(k), :]
        if r < 3 or (r == 3 and k == d):
            arrived(rs_in.at[d, r, part(k)], rss.at[d, r, k], rsr.at[d, r, k])
            value = value + rs_in[d, r, part(k), :].astype(F32)
        rs_out[d, r - 1, part(k), :] = value.astype(BF)
        send(
            rs_out.at[d, r - 1, part(k)], rs_in.at[d, r - 1, part(k)],
            rss.at[d, r - 1, k], rsr.at[d, r - 1, k], ring[d],
        )

    for d in (0, 1):
        rs_send(d, 3, 1 - d)
    gather_hop(4)
    block(7)
    for d in (0, 1):
        rs_send(d, 4, d)

    for i in (0, 1):
        total = d_audio[pl.ds(i * ROWS, ROWS), :]
        unit = units[i]
        share = (total - unit * jnp.sum(unit * total, axis=-1, keepdims=True)) / norms[i][:, 0:1]
        dp_low[pl.ds(i * ROWS, ROWS), :] = share.astype(BF)
        if i == 0:
            d_audio[pl.ds(0, ROWS), :] = share
    send(dp_low.at[pl.ds(ROWS, ROWS)], pair_dp, ps.at[2], pr.at[2], pair)

    for i in range(4):
        cut = pl.ds(i * 256, 256)
        grad_res[cut, :] = (
            lax.dot_general(audio[0, :, cut], dp_low[0:ROWS, :], (((0,), (0,)), ((), ())), preferred_element_type=F32)
            + lax.dot_general(audio[1, :, cut], dp_low[ROWS:, :], (((0,), (0,)), ((), ())), preferred_element_type=F32)
        ).astype(BF)
    store_grad = pltpu.make_async_copy(grad_res, grad_out, store_sem.at[2])
    store_grad.start()

    for d in (0, 1):
        rs_send(d, 3, d)
    for d in (0, 1):
        rs_send(d, 2, 1 - d)

    arrived(pair_dp, ps.at[2], pr.at[2])
    dproj = (d_audio[0:ROWS, :] + pair_dp[...].astype(F32)).astype(BF)
    audio_res[...] = lax.dot_general(
        dproj, weight[...].reshape(WIDE, COLS), (((1,), (1,)), ((), ())), preferred_element_type=F32
    ).astype(BF)
    store_audio = pltpu.make_async_copy(audio_res, audio_out, store_sem.at[0])
    store_audio.start()

    for d in (0, 1):
        rs_send(d, 2, d)
    for d in (0, 1):
        rs_send(d, 1, 1 - d)
    for d in (0, 1):
        rs_send(d, 1, d)
    for k in (0, 1):
        for d in (0, 1):
            arrived(rs_in.at[d, 0, part(k)], rss.at[d, 0, k], rsr.at[d, 0, k])
        total = d_text[0, part(k), :] + rs_in[0, 0, part(k), :].astype(F32) + rs_in[1, 0, part(k), :].astype(F32)
        raw = text[part(k), :].astype(F32)
        norm = jnp.sqrt(jnp.sum(raw * raw, axis=-1, keepdims=True) + EPS)
        unit = raw / norm
        text_res[part(k), :] = (
            (total - unit * jnp.sum(unit * total, axis=-1, keepdims=True)) / norm
        ).astype(BF)
    store_text = pltpu.make_async_copy(text_res, text_out, store_sem.at[1])
    store_text.start()
    for copy in started:
        copy.wait_send()
    store_grad.wait()
    store_audio.wait()
    store_text.wait()


def on_device(audio, text, labels, audio_weight):
    dma = pltpu.SemaphoreType.DMA
    audio_grad, text_grad, share = pl.pallas_call(
        kernel,
        out_shape=(
            jax.ShapeDtypeStruct((ROWS, WIDE), BF),
            jax.ShapeDtypeStruct((ROWS, COLS), BF),
            jax.ShapeDtypeStruct((WIDE, COLS), BF),
        ),
        in_specs=[
            pl.BlockSpec(memory_space=pl.ANY),
            pl.BlockSpec(memory_space=pl.ANY),
            pl.BlockSpec(memory_space=pltpu.VMEM),
            pl.BlockSpec(memory_space=pl.ANY),
        ],
        out_specs=[pl.BlockSpec(memory_space=pl.ANY)] * 3,
        scratch_shapes=[
            pltpu.VMEM((2, ROWS, WIDE), BF),
            pltpu.VMEM((ROWS, COLS), BF),
            pltpu.VMEM((8, ROWS, COLS), BF),
            pltpu.VMEM((8, 8, ROWS), F32),
            pltpu.VMEM((8, ROWS), F32),
            pltpu.VMEM((4, 8, 32, COLS), BF),
            pltpu.VMEM((2, ROWS, COLS), F32),
            pltpu.VMEM((2 * ROWS, COLS), BF),
            pltpu.VMEM((2, ROWS, 128), F32),
            pltpu.VMEM((2 * ROWS, COLS), F32),
            pltpu.VMEM((8, ROWS, COLS), F32),
            pltpu.VMEM((2 * ROWS, COLS), BF),
            pltpu.VMEM((ROWS, COLS), BF),
            pltpu.VMEM((2, 4, ROWS, COLS), BF),
            pltpu.VMEM((2, 4, ROWS, COLS), BF),
            pltpu.VMEM((ROWS, WIDE), BF),
            pltpu.VMEM((ROWS, COLS), BF),
            pltpu.VMEM((WIDE, COLS), BF),
            dma((3,)), dma((3,)),
            dma((2, 4, 2)), dma((2, 4, 2)),
            dma((2, 4)), dma((2, 4)),
            dma((3,)), dma((3,)),
            dma((3,)), dma((3,)),
            dma((4,)), dma((4,)),
            dma((3,)), dma((3,)),
            dma((2, 4, 2)), dma((2, 4, 2)),
        ],
        compiler_params=pltpu.CompilerParams(
            collective_id=0, has_side_effects=True, vmem_limit_bytes=48 * 2**20
        ),
    )(audio, text, labels.reshape(1, ROWS), audio_weight)
    grad = lax.psum_scatter(share, "group", scatter_dimension=0, tiled=True)
    weight_grad = lax.psum(grad, "blk").astype(F32)
    return (audio_grad, text_grad, weight_grad)


def solution(mesh):
    rows = P(("blk", "group"), None)
    return jax.shard_map(
        on_device,
        mesh=mesh,
        in_specs=(rows, rows, P(("blk", "group")), P("group", None)),
        out_specs=(rows, rows, P("group", None)),
        check_vma=False,
    )
```

```python
import jax
import jax.numpy as jnp
from jax import lax
from jax.experimental import pallas as pl
from jax.experimental.pallas import tpu as pltpu
from jax.sharding import PartitionSpec as P

MESH = pl.DeviceIdType.MESH
BF = jnp.bfloat16
F32 = jnp.float32
SCALE = 16.0
SHIFT = -4.0
EPS = 1e-6
ROWS, WIDE, COLS, HALF, MID = 160, 1024, 768, 80, 384


def kernel(
    audio_hbm, text_hbm, labels_hbm, weight_hbm,
    audio_out, text_out, grad_out,
    labels, audio, audio_other, text, texts, label_rows, pair_label, weight, units, unit_low, norms, d_audio, d_text,
    dp_low, dp_other, pair_dp, rs_out, rs_in, audio_res, text_res, grad_res,
    gx, gx_in, gz, gz_in, gy, gy_in, gf, gf_in,
    load_sem, store_sem, gs, gr, ls, lr, w1s, w1r, w2s, w2r, wcs, wcr, ps, pr, rss, rsr,
    cs, cr, xs, xr, zs, zr, ys, yr, fs, fr,
):
    blk, group = lax.axis_index("blk"), lax.axis_index("group")
    z_lo, y = blk // 8, blk % 8
    z_hi, x, core = group // 8, (group // 2) % 4, group % 2

    def at_y(step):
        return (z_lo * 8 + (y + step + 8) % 8, group)

    def at_x(step):
        return (blk, z_hi * 8 + ((x + step) % 4) * 2 + core)

    def at_z(step):
        return (blk, ((z_hi + step) % 4) * 8 + x * 2 + core)

    def at_z_all(step):
        there = (z_hi * 2 + z_lo + step) % 8
        return ((there % 2) * 8 + y, (there // 2) * 8 + x * 2 + core)

    pair = ((1 - z_lo) * 8 + y, group)
    other = (blk, z_hi * 8 + x * 2 + (1 - core))
    pair_other = ((1 - z_lo) * 8 + y, z_hi * 8 + x * 2 + (1 - core))
    ring = (at_y(1), at_y(-1))
    started = []

    def send(src, dst, s, r, to):
        copy = pltpu.make_async_remote_copy(
            src_ref=src, dst_ref=dst, send_sem=s, recv_sem=r, device_id=to, device_id_type=MESH
        )
        copy.start()
        started.append(copy)

    def arrived(dst, s, r):
        pltpu.make_async_remote_copy(
            src_ref=dst, dst_ref=dst, send_sem=s, recv_sem=r, device_id=ring[0], device_id_type=MESH
        ).wait_recv()

    loads = [
        pltpu.make_async_copy(text_hbm, text, load_sem.at[0]),
        pltpu.make_async_copy(weight_hbm, weight.at[z_hi, x * 2 + core], load_sem.at[1]),
        pltpu.make_async_copy(audio_hbm, audio.at[0], load_sem.at[2]),
        pltpu.make_async_copy(labels_hbm, labels, load_sem.at[3]),
    ]
    for load in loads:
        load.start()

    barrier = pltpu.get_barrier_semaphore()
    friends = ring + (pair, other) + tuple(at_z(i) for i in (1, 2, 3)) + tuple(at_x(i) for i in (1, 2, 3))
    for friend in friends:
        pl.semaphore_signal(barrier, inc=1, device_id=friend, device_id_type=MESH)

    loads[0].wait()
    raw = text[...].astype(F32)
    texts[0] = (raw / jnp.sqrt(jnp.sum(raw * raw, axis=-1, keepdims=True) + EPS)).astype(BF)
    loads[3].wait()
    label_rows[0] = jnp.broadcast_to(labels[...].reshape(1, ROWS).astype(F32), (8, ROWS))
    loads[1].wait()
    loads[2].wait()
    pl.semaphore_wait(barrier, len(friends))

    def part(k):
        return pl.ds(k * HALF, HALF)

    def slot_of(d, hop):
        return 2 * hop - 1 + d if hop < 4 else 7

    def gather_send(d, hop, k):
        src = 0 if hop == 1 else slot_of(d, hop - 1)
        send(
            texts.at[src, part(k)], texts.at[slot_of(d, hop), part(k)],
            gs.at[d, hop - 1, k], gr.at[d, hop - 1, k], ring[d],
        )

    def gather_wait(d, hop, k):
        arrived(texts.at[slot_of(d, hop), part(k)], gs.at[d, hop - 1, k], gr.at[d, hop - 1, k])

    def label_send(d, hop):
        src = 0 if hop == 1 else slot_of(d, hop - 1)
        send(
            label_rows.at[src], label_rows.at[slot_of(d, hop)],
            ls.at[d, hop - 1], lr.at[d, hop - 1], ring[d],
        )

    for k in (0, 1):
        for d in (0, 1):
            gather_send(d, 1, d if k == 0 else 1 - d)
    for d in (0, 1):
        label_send(d, 1)
    mine = weight.at[z_hi, x * 2 + core]
    for i in (1, 2, 3):
        send(mine, mine, w1s.at[i - 1], w1r.at[i - 1], at_z(i))
    send(label_rows.at[0], pair_label, ps.at[0], pr.at[0], pair)
    send(audio.at[0], audio.at[1], ps.at[1], pr.at[1], pair)
    send(audio.at[0], audio_other.at[0], cs.at[0], cr.at[0], other)

    def gather_hop(hop):
        for k in (0, 1):
            for d in (0, 1):
                which = d if k == 0 else 1 - d
                if hop == 4 and which != d:
                    continue
                gather_wait(d, hop, which)
                if hop < 3 or (hop == 3 and which == d):
                    gather_send(d, hop + 1, which)
        for d in (0, 1):
            if hop == 4 and d == 1:
                continue
            arrived(label_rows.at[slot_of(d, hop)], ls.at[d, hop - 1], lr.at[d, hop - 1])
            if hop < 3 or (hop == 3 and d == 0):
                label_send(d, hop + 1)

    gather_hop(1)
    for i in (1, 2, 3):
        there = weight.at[(z_hi + 4 - i) % 4, x * 2 + core]
        arrived(there, w1s.at[i - 1], w1r.at[i - 1])
    column = weight.at[:, x * 2 + core]
    for i in (1, 3, 2):
        send(column, column, w2s.at[i - 1], w2r.at[i - 1], at_x(i))
    send(column, column, wcs.at[0], wcr.at[0], other)
    gather_hop(2)
    for i in (1, 3, 2):
        there = weight.at[:, ((x + 4 - i) % 4) * 2 + core]
        arrived(there, w2s.at[i - 1], w2r.at[i - 1])
        send(there, there, wcs.at[i], wcr.at[i], other)
    gather_hop(3)
    for i in range(4):
        there = weight.at[:, ((x + 4 - i) % 4) * 2 + (1 - core)]
        arrived(there, wcs.at[i], wcr.at[i])
    arrived(pair_label, ps.at[0], pr.at[0])
    arrived(audio.at[1], ps.at[1], pr.at[1])
    send(audio.at[1], audio_other.at[1], cs.at[1], cr.at[1], other)

    whole = weight[...].reshape(WIDE, COLS)
    for i in (0, 1):
        proj = jnp.dot(audio[i], whole, preferred_element_type=F32)
        norm = jnp.sqrt(jnp.sum(proj * proj, axis=-1, keepdims=True) + EPS)
        unit = proj / norm
        units[i] = unit
        norms[i] = jnp.broadcast_to(norm, (ROWS, 128))
        unit_low[pl.ds(i * ROWS, ROWS)] = unit.astype(BF)

    diagonal = lax.broadcasted_iota(jnp.int32, (ROWS, ROWS), 0) == lax.broadcasted_iota(
        jnp.int32, (ROWS, ROWS), 1
    )

    def upright(row):
        return jnp.sum(jnp.where(diagonal, row, 0.0), axis=1, keepdims=True)

    own_labels = jnp.concatenate(
        [upright(label_rows[0][0:1, :]), upright(pair_label[...][0:1, :])], axis=0
    )

    d_audio[...] = jnp.zeros_like(d_audio)

    def block(slot):
        rows = texts[slot]
        logits = SCALE * lax.dot_general(
            unit_low[...], rows, (((1,), (1,)), ((), ())), preferred_element_type=F32
        ) + SHIFT
        positive = (own_labels == label_rows[slot][0:1, :]).astype(F32)
        pairs = (SCALE * (jax.nn.sigmoid(logits) - positive)).astype(BF)
        d_audio[...] += jnp.dot(pairs, rows, preferred_element_type=F32)
        d_text[slot] = lax.dot_general(
            pairs, unit_low[...], (((0,), (0,)), ((), ())), preferred_element_type=F32
        )

    def body(slot, carry):
        block(slot)
        return carry

    lax.fori_loop(0, 7, body, 0)

    def rs_send(d, r, k):
        slot = 7 if r == 4 else (2 * r if d == 0 else 2 * r - 1)
        value = d_text[slot, part(k), :]
        if r < 3 or (r == 3 and k == d):
            arrived(rs_in.at[d, r, part(k)], rss.at[d, r, k], rsr.at[d, r, k])
            value = value + rs_in[d, r, part(k), :].astype(F32)
        rs_out[d, r - 1, part(k), :] = value.astype(BF)
        send(
            rs_out.at[d, r - 1, part(k)], rs_in.at[d, r - 1, part(k)],
            rss.at[d, r - 1, k], rsr.at[d, r - 1, k], ring[d],
        )

    for d in (0, 1):
        rs_send(d, 3, 1 - d)
    gather_hop(4)
    block(7)
    for d in (0, 1):
        rs_send(d, 4, d)

    for i in (0, 1):
        total = d_audio[pl.ds(i * ROWS, ROWS), :]
        unit = units[i]
        share = (total - unit * jnp.sum(unit * total, axis=-1, keepdims=True)) / norms[i][:, 0:1]
        dp_low[0, i] = share[:, :MID].astype(BF)
        dp_low[1, i] = share[:, MID:].astype(BF)
        if i == 0:
            d_audio[pl.ds(0, ROWS), :] = share
    send(dp_low.at[1 - core], dp_other, cs.at[2], cr.at[2], other)
    send(dp_low.at[:, 1], pair_dp, ps.at[2], pr.at[2], pair)
    for i in (0, 1):
        arrived(audio_other.at[i], cs.at[i], cr.at[i])
    arrived(dp_other, cs.at[2], cr.at[2])

    for j in range(3):
        cut = pl.ds(j * 128, 128)
        total = jnp.zeros((WIDE, 128), F32)
        for rows, cols in ((audio, dp_low.at[core]), (audio_other, dp_other)):
            for i in (0, 1):
                total += lax.dot_general(
                    rows[i], cols[i, :, cut], (((0,), (0,)), ((), ())), preferred_element_type=F32
                )
        gx[j] = total.astype(BF).reshape(4, 4, 64, 128)
        for i in (1, 3, 2):
            send(gx.at[j, :, (x + i) % 4], gx_in.at[j, i - 1], xs.at[j, i - 1], xr.at[j, i - 1], at_x(i))

    for d in (0, 1):
        rs_send(d, 3, d)
    for d in (0, 1):
        rs_send(d, 2, 1 - d)

    arrived(pair_dp, ps.at[2], pr.at[2])
    both = jnp.concatenate([pair_dp[0], pair_dp[1]], axis=1).astype(F32)
    dproj = (d_audio[0:ROWS, :] + both).astype(BF)
    audio_res[...] = lax.dot_general(
        dproj, weight[...].reshape(WIDE, COLS), (((1,), (1,)), ((), ())), preferred_element_type=F32
    ).astype(BF)
    store_audio = pltpu.make_async_copy(audio_res, audio_out, store_sem.at[0])
    store_audio.start()

    for d in (0, 1):
        rs_send(d, 2, d)
    for d in (0, 1):
        rs_send(d, 1, 1 - d)
    for j in range(3):
        total = gx[j, :, x].astype(F32)
        for i in (1, 3, 2):
            arrived(gx_in.at[j, i - 1], xs.at[j, i - 1], xr.at[j, i - 1])
            total += gx_in[j, i - 1].astype(F32)
        gz[:, :, j] = total.astype(BF).reshape(4, 2, 32, 128)
    for i in (1, 7, 2, 6, 3, 5, 4):
        there = (z_hi * 2 + z_lo + i) % 8
        send(gz.at[there // 2, there % 2], gz_in.at[i - 1], zs.at[i - 1], zr.at[i - 1], at_z_all(i))
    for d in (0, 1):
        rs_send(d, 1, d)
    for k in (0, 1):
        for d in (0, 1):
            arrived(rs_in.at[d, 0, part(k)], rss.at[d, 0, k], rsr.at[d, 0, k])
        total = d_text[0, part(k), :] + rs_in[0, 0, part(k), :].astype(F32) + rs_in[1, 0, part(k), :].astype(F32)
        raw = text[part(k), :].astype(F32)
        norm = jnp.sqrt(jnp.sum(raw * raw, axis=-1, keepdims=True) + EPS)
        unit = raw / norm
        text_res[part(k), :] = (
            (total - unit * jnp.sum(unit * total, axis=-1, keepdims=True)) / norm
        ).astype(BF)
    store_text = pltpu.make_async_copy(text_res, text_out, store_sem.at[1])
    store_text.start()

    total = gz[z_hi, z_lo].astype(F32)
    for i in (1, 7, 2, 6, 3, 5, 4):
        arrived(gz_in.at[i - 1], zs.at[i - 1], zr.at[i - 1])
        total += gz_in[i - 1].astype(F32)
    gy[...] = total.astype(BF)
    for i in (1, 7, 2, 6, 3, 5, 4):
        send(gy, gy_in.at[i - 1], ys.at[i - 1], yr.at[i - 1], at_y(i))
    for i in (1, 7, 2, 6, 3, 5, 4):
        arrived(gy_in.at[i - 1], ys.at[i - 1], yr.at[i - 1])
        total += gy_in[i - 1].astype(F32)
    gf[...] = total.astype(BF)

    def final(to, k):
        return pltpu.make_async_remote_copy(
            src_ref=gf, dst_ref=gf_in.at[core], send_sem=fs.at[k], recv_sem=fr.at[core],
            device_id=to, device_id_type=MESH,
        )

    def landed(half):
        arrived(gf_in.at[half], fs.at[0], fr.at[half])

    @pl.when(core == z_lo)
    def _():
        copy = final(pair, 0)
        copy.start()
        gf_in[core] = gf[...]
        landed(1 - core)
        copy.wait_send()

    @pl.when(core != z_lo)
    def _():
        copy = final(pair_other, 0)
        copy.start()
        near = final(other, 1)
        near.start()
        landed(0)
        landed(1)
        copy.wait_send()
        near.wait_send()

    for half in (0, 1):
        for j in range(3):
            grad_res[:, pl.ds(half * MID + j * 128, 128)] = gf_in[half, j].astype(F32)
    store_grad = pltpu.make_async_copy(grad_res, grad_out, store_sem.at[2])
    store_grad.start()
    for copy in started:
        copy.wait_send()
    store_grad.wait()
    store_audio.wait()
    store_text.wait()


def on_device(audio, text, labels, audio_weight):
    dma = pltpu.SemaphoreType.DMA
    return pl.pallas_call(
        kernel,
        out_shape=(
            jax.ShapeDtypeStruct((ROWS, WIDE), BF),
            jax.ShapeDtypeStruct((ROWS, COLS), BF),
            jax.ShapeDtypeStruct((32, COLS), F32),
        ),
        in_specs=[pl.BlockSpec(memory_space=pltpu.HBM)] * 4,
        out_specs=[pl.BlockSpec(memory_space=pltpu.HBM)] * 3,
        scratch_shapes=[
            pltpu.VMEM((ROWS,), jnp.int32),
            pltpu.VMEM((2, ROWS, WIDE), BF),
            pltpu.VMEM((2, ROWS, WIDE), BF),
            pltpu.VMEM((ROWS, COLS), BF),
            pltpu.VMEM((8, ROWS, COLS), BF),
            pltpu.VMEM((8, 8, ROWS), F32),
            pltpu.VMEM((8, ROWS), F32),
            pltpu.VMEM((4, 8, 32, COLS), BF),
            pltpu.VMEM((2, ROWS, COLS), F32),
            pltpu.VMEM((2 * ROWS, COLS), BF),
            pltpu.VMEM((2, ROWS, 128), F32),
            pltpu.VMEM((2 * ROWS, COLS), F32),
            pltpu.VMEM((8, ROWS, COLS), F32),
            pltpu.VMEM((2, 2, ROWS, MID), BF),
            pltpu.VMEM((2, ROWS, MID), BF),
            pltpu.VMEM((2, ROWS, MID), BF),
            pltpu.VMEM((2, 4, ROWS, COLS), BF),
            pltpu.VMEM((2, 4, ROWS, COLS), BF),
            pltpu.VMEM((ROWS, WIDE), BF),
            pltpu.VMEM((ROWS, COLS), BF),
            pltpu.VMEM((32, COLS), F32),
            pltpu.VMEM((3, 4, 4, 64, 128), BF),
            pltpu.VMEM((3, 3, 4, 64, 128), BF),
            pltpu.VMEM((4, 2, 3, 32, 128), BF),
            pltpu.VMEM((7, 3, 32, 128), BF),
            pltpu.VMEM((3, 32, 128), BF),
            pltpu.VMEM((7, 3, 32, 128), BF),
            pltpu.VMEM((3, 32, 128), BF),
            pltpu.VMEM((2, 3, 32, 128), BF),
            dma((4,)), dma((3,)),
            dma((2, 4, 2)), dma((2, 4, 2)),
            dma((2, 4)), dma((2, 4)),
            dma((3,)), dma((3,)),
            dma((3,)), dma((3,)),
            dma((4,)), dma((4,)),
            dma((3,)), dma((3,)),
            dma((2, 4, 2)), dma((2, 4, 2)),
            dma((3,)), dma((3,)),
            dma((3, 3)), dma((3, 3)),
            dma((7,)), dma((7,)),
            dma((7,)), dma((7,)),
            dma((2,)), dma((2,)),
        ],
        compiler_params=pltpu.CompilerParams(
            collective_id=0, has_side_effects=True, vmem_limit_bytes=56 * 2**20
        ),
    )(audio, text, labels, audio_weight)


def solution(mesh):
    rows = P(("blk", "group"), None)
    return jax.shard_map(
        on_device,
        mesh=mesh,
        in_specs=(rows, rows, P(("blk", "group")), P("group", None)),
        out_specs=(rows, rows, P("group", None)),
        check_vma=False,
    )
```

```python
import jax
import jax.numpy as jnp
from jax import lax
from jax.experimental import pallas as pl
from jax.experimental.pallas import tpu as pltpu
from jax.sharding import PartitionSpec as P

MESH = pl.DeviceIdType.MESH
BF = jnp.bfloat16
F32 = jnp.float32
SCALE = 16.0
SHIFT = -4.0
EPS = 1e-6
ROWS, WIDE, COLS, HALF, MID = 160, 1024, 768, 80, 384
AROUND = (1, 7, 2, 6, 3, 5, 4)


def rows_by_columns(a, b):
    return lax.dot_general(a, b, (((1,), (1,)), ((), ())), preferred_element_type=F32)


def kernel(
    audio_hbm, text_hbm, labels_hbm, weight_hbm,
    audio_out, text_out, grad_out,
    labels, audio, audio_t, text, texts, label_rows, label_cols, pair_label, weight, units, unit_low, norms,
    d_audio, d_text, dp_low, dp_other, pair_dp, rs_out, rs_in, audio_res, text_res, grad_res,
    gx, gx_in, gz, gz_in, hz, hz_in, hx, hx_in, gy, gy_in, gf, gf_in,
    load_sem, store_sem, gs, gr, ls, lr, w1s, w1r, w2s, w2r, wcs, wcr, ps, pr, rss, rsr,
    cs, cr, xs, xr, zs, zr, hzs, hzr, hxs, hxr, ys, yr, fs, fr,
):
    blk, group = lax.axis_index("blk"), lax.axis_index("group")
    z_lo, y = blk // 8, blk % 8
    z_hi, x, core = group // 8, (group // 2) % 4, group % 2

    def at_y(step):
        return (z_lo * 8 + (y + step + 8) % 8, group)

    def at_x(step):
        return (blk, z_hi * 8 + ((x + step) % 4) * 2 + core)

    def at_z(step):
        there = (z_hi * 2 + z_lo + step + 8) % 8
        return ((there % 2) * 8 + y, (there // 2) * 8 + x * 2 + core)

    pair = ((1 - z_lo) * 8 + y, group)
    other = (blk, z_hi * 8 + x * 2 + (1 - core))
    pair_other = ((1 - z_lo) * 8 + y, z_hi * 8 + x * 2 + (1 - core))
    ring = (at_y(1), at_y(-1))
    started = []

    def send(src, dst, s, r, to):
        copy = pltpu.make_async_remote_copy(
            src_ref=src, dst_ref=dst, send_sem=s, recv_sem=r, device_id=to, device_id_type=MESH
        )
        copy.start()
        started.append(copy)

    def arrived(dst, s, r):
        pltpu.make_async_remote_copy(
            src_ref=dst, dst_ref=dst, send_sem=s, recv_sem=r, device_id=ring[0], device_id_type=MESH
        ).wait_recv()

    loads = [
        pltpu.make_async_copy(text_hbm, text, load_sem.at[0]),
        pltpu.make_async_copy(weight_hbm, weight.at[z_hi, x * 2 + core], load_sem.at[1]),
        pltpu.make_async_copy(labels_hbm, labels, load_sem.at[3]),
        pltpu.make_async_copy(audio_hbm, audio.at[0], load_sem.at[2]),
    ]
    for load in loads:
        load.start()

    barrier = pltpu.get_barrier_semaphore()
    away = 2 * z_lo - 1
    friends = ring + (pair, other, at_z(away), at_z(-2 * away), at_z(3 * away)) + tuple(at_x(i) for i in (1, 2, 3))
    for friend in friends:
        pl.semaphore_signal(barrier, inc=1, device_id=friend, device_id_type=MESH)

    loads[0].wait()
    raw = text[...].astype(F32)
    texts[0] = (raw / jnp.sqrt(jnp.sum(raw * raw, axis=-1, keepdims=True) + EPS)).astype(BF)
    loads[2].wait()
    label_rows[0] = jnp.broadcast_to(labels[...].reshape(1, ROWS).astype(F32), (8, ROWS))
    loads[1].wait()
    loads[3].wait()
    pl.semaphore_wait(barrier, len(friends))

    def part(k):
        return pl.ds(k * HALF, HALF)

    def slot_of(d, hop):
        return 2 * hop - 1 + d if hop < 4 else 7

    def gather_send(d, hop, k):
        src = 0 if hop == 1 else slot_of(d, hop - 1)
        send(
            texts.at[src, part(k)], texts.at[slot_of(d, hop), part(k)],
            gs.at[d, hop - 1, k], gr.at[d, hop - 1, k], ring[d],
        )

    def label_send(d, hop):
        src = 0 if hop == 1 else slot_of(d, hop - 1)
        send(
            label_rows.at[src], label_rows.at[slot_of(d, hop)],
            ls.at[d, hop - 1], lr.at[d, hop - 1], ring[d],
        )

    def gather_hop(hop, turn):
        for d in (0, 1):
            k = d if turn == 0 else 1 - d
            arrived(texts.at[slot_of(d, hop), part(k)], gs.at[d, hop - 1, k], gr.at[d, hop - 1, k])
            if hop < 3 or (hop == 3 and turn == 0):
                gather_send(d, hop + 1, k)

    diagonal = lax.broadcasted_iota(jnp.int32, (ROWS, ROWS), 0) == lax.broadcasted_iota(
        jnp.int32, (ROWS, ROWS), 1
    )

    def label_column(slot):
        row = label_rows[slot][0:1, :]
        column = jnp.sum(jnp.where(diagonal, row, 0.0), axis=1, keepdims=True)
        label_cols[slot] = jnp.broadcast_to(column, (ROWS, 128))

    def label_hop(hop):
        for d in (0, 1):
            if hop == 4 and d == 1:
                continue
            arrived(label_rows.at[slot_of(d, hop)], ls.at[d, hop - 1], lr.at[d, hop - 1])
            if hop < 3 or (hop == 3 and d == 0):
                label_send(d, hop + 1)
            label_column(slot_of(d, hop))

    def near_weight(e, i, side=core):
        return weight.at[(z_hi + 4 + away * (0, 1, -1, 2)[e]) % 4, ((x + 4 - i) % 4) * 2 + side]

    def weight_along_x(e):
        for i in (1, 3, 2):
            send(near_weight(e, 0), near_weight(e, 0), w2s.at[e, i - 1], w2r.at[e, i - 1], at_x(i))
        send(near_weight(e, 0), near_weight(e, 0), wcs.at[e, 0], wcr.at[e, 0], other)

    def weight_from_z(e):
        arrived(near_weight(e, 0), w1s.at[e - 1], w1r.at[e - 1])
        weight_along_x(e)

    def weight_from_x(e):
        for i in (1, 3, 2):
            there = near_weight(e, i)
            arrived(there, w2s.at[e, i - 1], w2r.at[e, i - 1])
            send(there, there, wcs.at[e, i], wcr.at[e, i], other)

    for d in (0, 1):
        gather_send(d, 1, d)
    mine = near_weight(0, 0)
    for e in (3, 2, 1):
        send(mine, mine, w1s.at[e - 1], w1r.at[e - 1], at_z(away * e))
    weight_along_x(0)
    for d in (0, 1):
        gather_send(d, 1, 1 - d)
        label_send(d, 1)
    send(label_rows.at[0], pair_label, ps.at[0], pr.at[0], pair)
    send(audio.at[0], audio.at[1], ps.at[1], pr.at[1], pair)
    send(audio.at[0], audio.at[2], cs.at[0], cr.at[0], other)
    label_column(0)
    audio_t[0] = audio[0].T

    gather_hop(1, 0)
    weight_from_z(1)
    weight_from_z(2)
    gather_hop(1, 1)
    weight_from_z(3)
    label_hop(1)
    weight_from_x(0)
    arrived(audio.at[2], cs.at[0], cr.at[0])
    audio_t[2] = audio[2].T
    gather_hop(2, 0)
    weight_from_x(1)
    weight_from_x(2)
    label_hop(2)
    gather_hop(2, 1)
    weight_from_x(3)
    arrived(pair_label, ps.at[0], pr.at[0])
    arrived(audio.at[1], ps.at[1], pr.at[1])
    send(audio.at[1], audio.at[3], cs.at[1], cr.at[1], other)
    audio_t[1] = audio[1].T
    gather_hop(3, 0)
    for e in range(4):
        for i in range(4):
            arrived(near_weight(e, i, 1 - core), wcs.at[e, i], wcr.at[e, i])

    whole = weight[...].reshape(WIDE, COLS)
    for i in (0, 1):
        proj = jnp.dot(audio[i], whole, preferred_element_type=F32)
        norm = jnp.sqrt(jnp.sum(proj * proj, axis=-1, keepdims=True) + EPS)
        unit = proj / norm
        units[i] = unit
        norms[i] = jnp.broadcast_to(norm, (ROWS, 128))
        unit_low[i] = unit.astype(BF)

    def blocks(first, count):
        many = count * ROWS
        rows = texts[first : first + count].reshape(many, COLS)
        row_labels = label_cols[first : first + count].reshape(many, 128)[:, 0:1]
        more = jnp.zeros((many, COLS), F32)
        for i in (0, 1):
            logits = SCALE * rows_by_columns(rows, unit_low[i]) + SHIFT
            own = label_rows[0][0:1, :] if i == 0 else pair_label[0:1, :]
            positive = (row_labels == own).astype(F32)
            pairs = (SCALE * (jax.nn.sigmoid(logits) - positive)).astype(BF)
            part_sum = lax.dot_general(pairs, rows, (((0,), (0,)), ((), ())), preferred_element_type=F32)
            d_audio[i] = part_sum if first == 0 else d_audio[i] + part_sum
            more += jnp.dot(pairs, unit_low[i], preferred_element_type=F32)
        d_text[first : first + count] = more.reshape(count, ROWS, COLS)

    def rs_send(r, turn):
        for d in (0, 1):
            k = d if turn == 0 else 1 - d
            slot = 7 if r == 4 else (2 * r if d == 0 else 2 * r - 1)
            value = d_text[slot, part(k), :]
            if r < 3 or (r == 3 and turn == 0):
                arrived(rs_in.at[d, r, part(k)], rss.at[d, r, k], rsr.at[d, r, k])
                value = value + rs_in[d, r, part(k), :].astype(F32)
            rs_out[d, r - 1, part(k), :] = value.astype(BF)
            send(
                rs_out.at[d, r - 1, part(k)], rs_in.at[d, r - 1, part(k)],
                rss.at[d, r - 1, k], rsr.at[d, r - 1, k], ring[d],
            )

    blocks(0, 3)
    label_hop(3)
    gather_hop(3, 1)
    blocks(3, 4)
    rs_send(3, 1)
    label_hop(4)
    arrived(audio.at[3], cs.at[1], cr.at[1])
    audio_t[3] = audio[3].T
    gather_hop(4, 0)
    blocks(7, 1)

    for i in (1, 0):
        total = d_audio[i]
        unit = units[i]
        share = (total - unit * jnp.sum(unit * total, axis=-1, keepdims=True)) / norms[i][:, 0:1]
        dp_low[0, i] = share[:, :MID].astype(BF)
        dp_low[1, i] = share[:, MID:].astype(BF)
        if i == 0:
            d_audio[0] = share
    send(dp_low.at[1 - core], dp_other, cs.at[2], cr.at[2], other)
    rs_send(4, 0)
    arrived(dp_other, cs.at[2], cr.at[2])

    def product(cut):
        total = jnp.dot(audio_t[0], dp_low[core, 0, :, cut], preferred_element_type=F32)
        total += jnp.dot(audio_t[1], dp_low[core, 1, :, cut], preferred_element_type=F32)
        total += jnp.dot(audio_t[2], dp_other[0, :, cut], preferred_element_type=F32)
        return total + jnp.dot(audio_t[3], dp_other[1, :, cut], preferred_element_type=F32)

    hz[...] = product(pl.ds(256, 128)).astype(BF).reshape(4, 4, 2, 32, 128)
    for i in AROUND:
        there = (z_hi * 2 + z_lo + i) % 8
        send(hz.at[there // 2, :, there % 2], hz_in.at[i - 1], hzs.at[i - 1], hzr.at[i - 1], at_z(i))
    for j in (0, 1):
        gx[j] = product(pl.ds(j * 128, 128)).astype(BF).reshape(4, 4, 64, 128)
        for i in (2, 1, 3):
            send(gx.at[j, :, (x + i) % 4], gx_in.at[j, i - 1], xs.at[j, i - 1], xr.at[j, i - 1], at_x(i))

    def along_z(j):
        total = gx[j, :, x].astype(F32)
        for i in (1, 3, 2):
            arrived(gx_in.at[j, i - 1], xs.at[j, i - 1], xr.at[j, i - 1])
            total += gx_in[j, i - 1].astype(F32)
        gz[j] = total.astype(BF).reshape(4, 2, 32, 128)
        for i in AROUND:
            there = (z_hi * 2 + z_lo + i) % 8
            send(gz.at[j, there // 2, there % 2], gz_in.at[j, i - 1], zs.at[j, i - 1], zr.at[j, i - 1], at_z(i))

    def along_x():
        total = hz[z_hi, :, z_lo].astype(F32)
        for i in AROUND:
            arrived(hz_in.at[i - 1], hzs.at[i - 1], hzr.at[i - 1])
            total += hz_in[i - 1].astype(F32)
        hx[...] = total.astype(BF)
        for i in (2, 1, 3):
            send(hx.at[(x + i) % 4], hx_in.at[i - 1], hxs.at[i - 1], hxr.at[i - 1], at_x(i))

    def along_y(j):
        if j < 2:
            total = gz[j, z_hi, z_lo].astype(F32)
            for i in AROUND:
                arrived(gz_in.at[j, i - 1], zs.at[j, i - 1], zr.at[j, i - 1])
                total += gz_in[j, i - 1].astype(F32)
        else:
            total = hx[x].astype(F32)
            for i in (1, 3, 2):
                arrived(hx_in.at[i - 1], hxs.at[i - 1], hxr.at[i - 1])
                total += hx_in[i - 1].astype(F32)
        gy[j] = total.astype(BF)
        for i in AROUND:
            send(gy.at[j], gy_in.at[j, i - 1], ys.at[j, i - 1], yr.at[j, i - 1], at_y(i))

    def complete(j):
        total = gy[j].astype(F32)
        for i in AROUND:
            arrived(gy_in.at[j, i - 1], ys.at[j, i - 1], yr.at[j, i - 1])
            total += gy_in[j, i - 1].astype(F32)
        gf[j] = total.astype(BF)

    rs_send(2, 1)
    rs_send(3, 0)
    along_z(0)
    rs_send(1, 1)
    rs_send(2, 0)
    along_z(1)
    send(dp_low.at[:, 1], pair_dp, ps.at[2], pr.at[2], pair)
    along_x()

    along_y(0)
    along_y(2)
    rs_send(1, 0)
    along_y(1)

    for turn in (1, 0):
        for k in (0, 1):
            d = k if turn == 0 else 1 - k
            arrived(rs_in.at[d, 0, part(k)], rss.at[d, 0, k], rsr.at[d, 0, k])
    raw = text[...].astype(F32)
    norm = jnp.sqrt(jnp.sum(raw * raw, axis=-1, keepdims=True) + EPS)
    unit = raw / norm
    total = d_text[0] + rs_in[0, 0].astype(F32) + rs_in[1, 0].astype(F32)
    text_res[...] = ((total - unit * jnp.sum(unit * total, axis=-1, keepdims=True)) / norm).astype(BF)
    store_text = pltpu.make_async_copy(text_res, text_out, store_sem.at[1])
    store_text.start()

    arrived(pair_dp, ps.at[2], pr.at[2])
    both = jnp.concatenate([pair_dp[0], pair_dp[1]], axis=1).astype(F32)
    dproj = (d_audio[0] + both).astype(BF)
    audio_res[...] = rows_by_columns(dproj, weight[...].reshape(WIDE, COLS)).astype(BF)
    store_audio = pltpu.make_async_copy(audio_res, audio_out, store_sem.at[0])
    store_audio.start()

    complete(0)
    complete(2)
    complete(1)

    def final(to, k):
        return pltpu.make_async_remote_copy(
            src_ref=gf, dst_ref=gf_in.at[core], send_sem=fs.at[k], recv_sem=fr.at[core],
            device_id=to, device_id_type=MESH,
        )

    def landed(half):
        arrived(gf_in.at[half], fs.at[0], fr.at[half])

    @pl.when(core == z_lo)
    def _():
        copy = final(pair, 0)
        copy.start()
        gf_in[core] = gf[...]
        landed(1 - core)
        copy.wait_send()

    @pl.when(core != z_lo)
    def _():
        copy = final(pair_other, 0)
        copy.start()
        near = final(other, 1)
        near.start()
        landed(0)
        landed(1)
        copy.wait_send()
        near.wait_send()

    for half in (0, 1):
        for j in range(3):
            grad_res[:, pl.ds(half * MID + j * 128, 128)] = gf_in[half, j].astype(F32)
    store_grad = pltpu.make_async_copy(grad_res, grad_out, store_sem.at[2])
    store_grad.start()
    for copy in started:
        copy.wait_send()
    store_audio.wait()
    store_text.wait()
    store_grad.wait()


def on_device(audio, text, labels, audio_weight):
    dma = pltpu.SemaphoreType.DMA
    twice = lambda *shape: [dma(shape), dma(shape)]
    return pl.pallas_call(
        kernel,
        out_shape=(
            jax.ShapeDtypeStruct((ROWS, WIDE), BF),
            jax.ShapeDtypeStruct((ROWS, COLS), BF),
            jax.ShapeDtypeStruct((32, COLS), F32),
        ),
        in_specs=[pl.BlockSpec(memory_space=pltpu.HBM)] * 4,
        out_specs=[pl.BlockSpec(memory_space=pltpu.HBM)] * 3,
        scratch_shapes=[
            pltpu.VMEM((ROWS,), jnp.int32),
            pltpu.VMEM((4, ROWS, WIDE), BF),
            pltpu.VMEM((4, WIDE, ROWS), BF),
            pltpu.VMEM((ROWS, COLS), BF),
            pltpu.VMEM((8, ROWS, COLS), BF),
            pltpu.VMEM((8, 8, ROWS), F32),
            pltpu.VMEM((8, ROWS, 128), F32),
            pltpu.VMEM((8, ROWS), F32),
            pltpu.VMEM((4, 8, 32, COLS), BF),
            pltpu.VMEM((2, ROWS, COLS), F32),
            pltpu.VMEM((2, ROWS, COLS), BF),
            pltpu.VMEM((2, ROWS, 128), F32),
            pltpu.VMEM((2, ROWS, COLS), F32),
            pltpu.VMEM((8, ROWS, COLS), F32),
            pltpu.VMEM((2, 2, ROWS, MID), BF),
            pltpu.VMEM((2, ROWS, MID), BF),
            pltpu.VMEM((2, ROWS, MID), BF),
            pltpu.VMEM((2, 4, ROWS, COLS), BF),
            pltpu.VMEM((2, 4, ROWS, COLS), BF),
            pltpu.VMEM((ROWS, WIDE), BF),
            pltpu.VMEM((ROWS, COLS), BF),
            pltpu.VMEM((32, COLS), F32),
            pltpu.VMEM((2, 4, 4, 64, 128), BF),
            pltpu.VMEM((2, 3, 4, 64, 128), BF),
            pltpu.VMEM((2, 4, 2, 32, 128), BF),
            pltpu.VMEM((2, 7, 32, 128), BF),
            pltpu.VMEM((4, 4, 2, 32, 128), BF),
            pltpu.VMEM((7, 4, 32, 128), BF),
            pltpu.VMEM((4, 32, 128), BF),
            pltpu.VMEM((3, 32, 128), BF),
            pltpu.VMEM((3, 32, 128), BF),
            pltpu.VMEM((3, 7, 32, 128), BF),
            pltpu.VMEM((3, 32, 128), BF),
            pltpu.VMEM((2, 3, 32, 128), BF),
            dma((4,)), dma((3,)),
            *twice(2, 4, 2), *twice(2, 4),
            *twice(3), *twice(4, 3), *twice(4, 4),
            *twice(3), *twice(2, 4, 2),
            *twice(3), *twice(2, 3), *twice(2, 7), *twice(7), *twice(3), *twice(3, 7), *twice(2),
        ],
        compiler_params=pltpu.CompilerParams(
            collective_id=0, has_side_effects=True, vmem_limit_bytes=56 * 2**20
        ),
    )(audio, text, labels, audio_weight)


def solution(mesh):
    rows = P(("blk", "group"), None)
    return jax.shard_map(
        on_device,
        mesh=mesh,
        in_specs=(rows, rows, P(("blk", "group")), P("group", None)),
        out_specs=(rows, rows, P("group", None)),
        check_vma=False,
    )
```

```python
import jax
import jax.numpy as jnp
from jax import lax
from jax.experimental import pallas as pl
from jax.experimental.pallas import tpu as pltpu
from jax.sharding import PartitionSpec as P

MESH = pl.DeviceIdType.MESH
BF = jnp.bfloat16
F32 = jnp.float32
SCALE = 16.0
SHIFT = -4.0
EPS = 1e-6
ROWS, WIDE, COLS, HALF, MID = 160, 1024, 768, 80, 384
AROUND = (1, 7, 2, 6, 3, 5, 4)


def rows_by_columns(a, b):
    return lax.dot_general(a, b, (((1,), (1,)), ((), ())), preferred_element_type=F32)


def kernel(
    audio_hbm, text_hbm, labels_hbm, weight_hbm,
    audio_out, text_out, grad_out,
    labels, audio, audio_t, text, texts, label_rows, label_cols, pair_label, weight, units, unit_low, norms,
    d_audio, d_text, dp_low, dp_other, pair_dp, rs_out, rs_in, audio_res, text_res, grad_res,
    gx, gx_in, gz, gz_in, hz, hz_in, hx, hx_in, gy, gy_in, gf, gf_in,
    load_sem, store_sem, gs, gr, ls, lr, w1s, w1r, w2s, w2r, wcs, wcr, ps, pr, rss, rsr,
    cs, cr, xs, xr, zs, zr, hzs, hzr, hxs, hxr, ys, yr, fs, fr,
):
    blk, group = lax.axis_index("blk"), lax.axis_index("group")
    z_lo, y = blk // 8, blk % 8
    z_hi, x, core = group // 8, (group // 2) % 4, group % 2

    def at_y(step):
        return (z_lo * 8 + (y + step + 8) % 8, group)

    def at_x(step):
        return (blk, z_hi * 8 + ((x + step) % 4) * 2 + core)

    def at_z(step):
        there = (z_hi * 2 + z_lo + step + 8) % 8
        return ((there % 2) * 8 + y, (there // 2) * 8 + x * 2 + core)

    pair = ((1 - z_lo) * 8 + y, group)
    other = (blk, z_hi * 8 + x * 2 + (1 - core))
    pair_other = ((1 - z_lo) * 8 + y, z_hi * 8 + x * 2 + (1 - core))
    ring = (at_y(1), at_y(-1))
    started = []

    def send(src, dst, s, r, to):
        copy = pltpu.make_async_remote_copy(
            src_ref=src, dst_ref=dst, send_sem=s, recv_sem=r, device_id=to, device_id_type=MESH
        )
        copy.start()
        started.append(copy)

    def arrived(dst, s, r):
        pltpu.make_async_remote_copy(
            src_ref=dst, dst_ref=dst, send_sem=s, recv_sem=r, device_id=ring[0], device_id_type=MESH
        ).wait_recv()

    loads = [
        pltpu.make_async_copy(text_hbm, text, load_sem.at[0]),
        pltpu.make_async_copy(weight_hbm, weight.at[z_hi, x * 2 + core], load_sem.at[1]),
        pltpu.make_async_copy(labels_hbm, labels, load_sem.at[3]),
        pltpu.make_async_copy(audio_hbm, audio.at[0], load_sem.at[2]),
    ]
    for load in loads:
        load.start()

    barrier = pltpu.get_barrier_semaphore()
    away = 2 * z_lo - 1
    friends = ring + (pair, other, at_z(away), at_z(-2 * away), at_z(3 * away)) + tuple(at_x(i) for i in (1, 2, 3))
    for friend in friends:
        pl.semaphore_signal(barrier, inc=1, device_id=friend, device_id_type=MESH)

    loads[0].wait()
    raw = text[...].astype(F32)
    texts[0] = (raw / jnp.sqrt(jnp.sum(raw * raw, axis=-1, keepdims=True) + EPS)).astype(BF)
    loads[2].wait()
    label_rows[0] = jnp.broadcast_to(labels[...].reshape(1, ROWS).astype(F32), (8, ROWS))
    loads[1].wait()
    loads[3].wait()
    pl.semaphore_wait(barrier, len(friends))

    def part(k):
        return pl.ds(k * HALF, HALF)

    def slot_of(d, hop):
        return 2 * hop - 1 + d if hop < 4 else 7

    def gather_send(d, hop, k):
        src = 0 if hop == 1 else slot_of(d, hop - 1)
        send(
            texts.at[src, part(k)], texts.at[slot_of(d, hop), part(k)],
            gs.at[d, hop - 1, k], gr.at[d, hop - 1, k], ring[d],
        )

    def label_send(d, hop):
        src = 0 if hop == 1 else slot_of(d, hop - 1)
        send(
            label_rows.at[src], label_rows.at[slot_of(d, hop)],
            ls.at[d, hop - 1], lr.at[d, hop - 1], ring[d],
        )

    def gather_hop(hop, turn):
        for d in (0, 1):
            k = d if turn == 0 else 1 - d
            arrived(texts.at[slot_of(d, hop), part(k)], gs.at[d, hop - 1, k], gr.at[d, hop - 1, k])
            if hop < 3 or (hop == 3 and turn == 0):
                gather_send(d, hop + 1, k)

    diagonal = lax.broadcasted_iota(jnp.int32, (ROWS, ROWS), 0) == lax.broadcasted_iota(
        jnp.int32, (ROWS, ROWS), 1
    )

    def label_column(slot):
        row = label_rows[slot][0:1, :]
        column = jnp.sum(jnp.where(diagonal, row, 0.0), axis=1, keepdims=True)
        label_cols[slot] = jnp.broadcast_to(column, (ROWS, 128))

    def label_hop(hop):
        for d in (0, 1):
            if hop == 4 and d == 1:
                continue
            arrived(label_rows.at[slot_of(d, hop)], ls.at[d, hop - 1], lr.at[d, hop - 1])
            if hop < 3 or (hop == 3 and d == 0):
                label_send(d, hop + 1)
            label_column(slot_of(d, hop))

    def near_weight(e, i, side=core):
        return weight.at[(z_hi + 4 + away * (0, 1, -1, 2)[e]) % 4, ((x + 4 - i) % 4) * 2 + side]

    def weight_along_x(e):
        for i in (1, 3, 2):
            send(near_weight(e, 0), near_weight(e, 0), w2s.at[e, i - 1], w2r.at[e, i - 1], at_x(i))
        send(near_weight(e, 0), near_weight(e, 0), wcs.at[e, 0], wcr.at[e, 0], other)

    def weight_from_z(e):
        arrived(near_weight(e, 0), w1s.at[e - 1], w1r.at[e - 1])
        weight_along_x(e)

    def weight_from_x(e):
        for i in (1, 3, 2):
            there = near_weight(e, i)
            arrived(there, w2s.at[e, i - 1], w2r.at[e, i - 1])
            send(there, there, wcs.at[e, i], wcr.at[e, i], other)

    for d in (0, 1):
        gather_send(d, 1, d)
    mine = near_weight(0, 0)
    for e in (3, 2, 1):
        send(mine, mine, w1s.at[e - 1], w1r.at[e - 1], at_z(away * e))
    weight_along_x(0)
    for d in (0, 1):
        gather_send(d, 1, 1 - d)
        label_send(d, 1)
    send(label_rows.at[0], pair_label, ps.at[0], pr.at[0], pair)
    send(audio.at[0], audio.at[1], ps.at[1], pr.at[1], pair)
    send(audio.at[0], audio.at[2], cs.at[0], cr.at[0], other)
    label_column(0)
    audio_t[0] = audio[0].T

    gather_hop(1, 0)
    weight_from_z(1)
    weight_from_z(2)
    gather_hop(1, 1)
    weight_from_z(3)
    label_hop(1)
    weight_from_x(0)
    arrived(audio.at[2], cs.at[0], cr.at[0])
    audio_t[2] = audio[2].T
    gather_hop(2, 0)
    weight_from_x(1)
    weight_from_x(2)
    label_hop(2)
    gather_hop(2, 1)
    weight_from_x(3)
    arrived(pair_label, ps.at[0], pr.at[0])
    arrived(audio.at[1], ps.at[1], pr.at[1])
    send(audio.at[1], audio.at[3], cs.at[1], cr.at[1], other)
    audio_t[1] = audio[1].T
    gather_hop(3, 0)
    for e in range(4):
        for i in range(4):
            arrived(near_weight(e, i, 1 - core), wcs.at[e, i], wcr.at[e, i])

    whole = weight[...].reshape(WIDE, COLS)
    for i in (0, 1):
        proj = jnp.dot(audio[i], whole, preferred_element_type=F32)
        norm = jnp.sqrt(jnp.sum(proj * proj, axis=-1, keepdims=True) + EPS)
        unit = proj / norm
        units[i] = unit
        norms[i] = jnp.broadcast_to(norm, (ROWS, 128))
        unit_low[i] = unit.astype(BF)

    def blocks(first, count):
        many = count * ROWS
        rows = texts[first : first + count].reshape(many, COLS)
        row_labels = label_cols[first : first + count].reshape(many, 128)[:, 0:1]
        pairs = []
        for i in (0, 1):
            logits = SCALE * rows_by_columns(rows, unit_low[i]) + SHIFT
            own = label_rows[0][0:1, :] if i == 0 else pair_label[0:1, :]
            positive = (row_labels == own).astype(F32)
            pairs.append((SCALE * (jax.nn.sigmoid(logits) - positive)).astype(BF))
        d_text[first : first + count] = (
            jnp.dot(pairs[0], unit_low[0], preferred_element_type=F32)
            + jnp.dot(pairs[1], unit_low[1], preferred_element_type=F32)
        ).reshape(count, ROWS, COLS)
        for i in (0, 1):
            more = lax.dot_general(pairs[i], rows, (((0,), (0,)), ((), ())), preferred_element_type=F32)
            d_audio[i] = more if first == 0 else d_audio[i] + more

    def rs_send(r, turn):
        for d in (0, 1):
            k = d if turn == 0 else 1 - d
            slot = 7 if r == 4 else (2 * r if d == 0 else 2 * r - 1)
            value = d_text[slot, part(k), :]
            if r < 3 or (r == 3 and turn == 0):
                arrived(rs_in.at[d, r, part(k)], rss.at[d, r, k], rsr.at[d, r, k])
                value = value + rs_in[d, r, part(k), :].astype(F32)
            rs_out[d, r - 1, part(k), :] = value.astype(BF)
            send(
                rs_out.at[d, r - 1, part(k)], rs_in.at[d, r - 1, part(k)],
                rss.at[d, r - 1, k], rsr.at[d, r - 1, k], ring[d],
            )

    blocks(0, 3)
    label_hop(3)
    gather_hop(3, 1)
    blocks(3, 4)
    rs_send(3, 1)
    label_hop(4)
    arrived(audio.at[3], cs.at[1], cr.at[1])
    audio_t[3] = audio[3].T
    gather_hop(4, 0)
    blocks(7, 1)
    rs_send(4, 0)

    for i in (1, 0):
        total = d_audio[i]
        unit = units[i]
        share = (total - unit * jnp.sum(unit * total, axis=-1, keepdims=True)) / norms[i][:, 0:1]
        dp_low[0, i] = share[:, :MID].astype(BF)
        dp_low[1, i] = share[:, MID:].astype(BF)
        if i == 0:
            d_audio[0] = share
    send(dp_low.at[1 - core], dp_other, cs.at[2], cr.at[2], other)
    arrived(dp_other, cs.at[2], cr.at[2])

    def product(cut):
        total = jnp.dot(audio_t[0], dp_low[core, 0, :, cut], preferred_element_type=F32)
        total += jnp.dot(audio_t[1], dp_low[core, 1, :, cut], preferred_element_type=F32)
        total += jnp.dot(audio_t[2], dp_other[0, :, cut], preferred_element_type=F32)
        return total + jnp.dot(audio_t[3], dp_other[1, :, cut], preferred_element_type=F32)

    first = product(pl.ds(0, 256)).astype(BF)
    for j in (0, 1):
        gx[j] = first[:, j * 128 : j * 128 + 128].reshape(4, 4, 64, 128)
        for i in (2, 1, 3):
            send(gx.at[j, :, (x + i) % 4], gx_in.at[j, i - 1], xs.at[j, i - 1], xr.at[j, i - 1], at_x(i))
    hz[...] = product(pl.ds(256, 128)).astype(BF).reshape(4, 4, 2, 32, 128)
    for i in AROUND:
        there = (z_hi * 2 + z_lo + i) % 8
        send(hz.at[there // 2, :, there % 2], hz_in.at[i - 1], hzs.at[i - 1], hzr.at[i - 1], at_z(i))

    def along_z(j):
        total = gx[j, :, x].astype(F32)
        for i in (1, 3, 2):
            arrived(gx_in.at[j, i - 1], xs.at[j, i - 1], xr.at[j, i - 1])
            total += gx_in[j, i - 1].astype(F32)
        gz[j] = total.astype(BF).reshape(4, 2, 32, 128)
        for i in AROUND:
            there = (z_hi * 2 + z_lo + i) % 8
            send(gz.at[j, there // 2, there % 2], gz_in.at[j, i - 1], zs.at[j, i - 1], zr.at[j, i - 1], at_z(i))

    def along_x():
        total = hz[z_hi, :, z_lo].astype(F32)
        for i in AROUND:
            arrived(hz_in.at[i - 1], hzs.at[i - 1], hzr.at[i - 1])
            total += hz_in[i - 1].astype(F32)
        hx[...] = total.astype(BF)
        for i in (2, 1, 3):
            send(hx.at[(x + i) % 4], hx_in.at[i - 1], hxs.at[i - 1], hxr.at[i - 1], at_x(i))

    def along_y(j):
        if j < 2:
            total = gz[j, z_hi, z_lo].astype(F32)
            for i in AROUND:
                arrived(gz_in.at[j, i - 1], zs.at[j, i - 1], zr.at[j, i - 1])
                total += gz_in[j, i - 1].astype(F32)
        else:
            total = hx[x].astype(F32)
            for i in (1, 3, 2):
                arrived(hx_in.at[i - 1], hxs.at[i - 1], hxr.at[i - 1])
                total += hx_in[i - 1].astype(F32)
        gy[j] = total.astype(BF)
        for i in AROUND:
            send(gy.at[j], gy_in.at[j, i - 1], ys.at[j, i - 1], yr.at[j, i - 1], at_y(i))

    def complete(j):
        total = gy[j].astype(F32)
        for i in AROUND:
            arrived(gy_in.at[j, i - 1], ys.at[j, i - 1], yr.at[j, i - 1])
            total += gy_in[j, i - 1].astype(F32)
        gf[j] = total.astype(BF)

    rs_send(2, 1)
    rs_send(3, 0)
    along_z(0)
    along_z(1)
    send(dp_low.at[:, 1], pair_dp, ps.at[2], pr.at[2], pair)
    rs_send(1, 1)
    rs_send(2, 0)
    along_x()
    along_y(0)
    along_y(2)
    along_y(1)
    rs_send(1, 0)

    complete(0)
    complete(2)
    complete(1)

    def final(to, k):
        return pltpu.make_async_remote_copy(
            src_ref=gf, dst_ref=gf_in.at[core], send_sem=fs.at[k], recv_sem=fr.at[core],
            device_id=to, device_id_type=MESH,
        )

    def landed(half):
        arrived(gf_in.at[half], fs.at[0], fr.at[half])

    @pl.when(core == z_lo)
    def _():
        final(pair, 0).start()
        gf_in[core] = gf[...]

    @pl.when(core != z_lo)
    def _():
        final(pair_other, 0).start()
        final(other, 1).start()

    arrived(pair_dp, ps.at[2], pr.at[2])
    both = jnp.concatenate([pair_dp[0], pair_dp[1]], axis=1).astype(F32)
    dproj = (d_audio[0] + both).astype(BF)
    audio_res[...] = rows_by_columns(dproj, weight[...].reshape(WIDE, COLS)).astype(BF)
    store_audio = pltpu.make_async_copy(audio_res, audio_out, store_sem.at[0])
    store_audio.start()

    for turn in (1, 0):
        for k in (0, 1):
            d = k if turn == 0 else 1 - k
            arrived(rs_in.at[d, 0, part(k)], rss.at[d, 0, k], rsr.at[d, 0, k])
    raw = text[...].astype(F32)
    norm = jnp.sqrt(jnp.sum(raw * raw, axis=-1, keepdims=True) + EPS)
    unit = raw / norm
    total = d_text[0] + rs_in[0, 0].astype(F32) + rs_in[1, 0].astype(F32)
    text_res[...] = ((total - unit * jnp.sum(unit * total, axis=-1, keepdims=True)) / norm).astype(BF)
    store_text = pltpu.make_async_copy(text_res, text_out, store_sem.at[1])
    store_text.start()

    @pl.when(core == z_lo)
    def _():
        landed(1 - core)
        final(pair, 0).wait_send()

    @pl.when(core != z_lo)
    def _():
        landed(0)
        landed(1)
        final(pair_other, 0).wait_send()
        final(other, 1).wait_send()

    for half in (0, 1):
        for j in range(3):
            grad_res[:, pl.ds(half * MID + j * 128, 128)] = gf_in[half, j].astype(F32)
    store_grad = pltpu.make_async_copy(grad_res, grad_out, store_sem.at[2])
    store_grad.start()
    for copy in started:
        copy.wait_send()
    store_audio.wait()
    store_text.wait()
    store_grad.wait()


def hand_over(audio_in, text_in, grad_in, audio_out, text_out, grad_out, audio, text, grad, sems):
    ways = ((audio_in, audio, audio_out), (text_in, text, text_out), (grad_in, grad, grad_out))
    loads = [pltpu.make_async_copy(src, by, sems.at[i]) for i, (src, by, _) in enumerate(ways)]
    stores = [pltpu.make_async_copy(by, dst, sems.at[3 + i]) for i, (_, by, dst) in enumerate(ways)]
    for load in loads:
        load.start()
    for load, store in zip(loads, stores):
        load.wait()
        store.start()
    for store in stores:
        store.wait()


def on_device(audio, text, labels, audio_weight):
    dma = pltpu.SemaphoreType.DMA
    twice = lambda *shape: [dma(shape), dma(shape)]
    shapes = (
        jax.ShapeDtypeStruct((ROWS, WIDE), BF),
        jax.ShapeDtypeStruct((ROWS, COLS), BF),
        jax.ShapeDtypeStruct((32, COLS), F32),
    )
    results = pl.pallas_call(
        kernel,
        out_shape=shapes,
        in_specs=[pl.BlockSpec(memory_space=pltpu.HBM)] * 4,
        out_specs=[pl.BlockSpec(memory_space=pltpu.HBM)] * 3,
        scratch_shapes=[
            pltpu.VMEM((ROWS,), jnp.int32),
            pltpu.VMEM((4, ROWS, WIDE), BF),
            pltpu.VMEM((4, WIDE, ROWS), BF),
            pltpu.VMEM((ROWS, COLS), BF),
            pltpu.VMEM((8, ROWS, COLS), BF),
            pltpu.VMEM((8, 8, ROWS), F32),
            pltpu.VMEM((8, ROWS, 128), F32),
            pltpu.VMEM((8, ROWS), F32),
            pltpu.VMEM((4, 8, 32, COLS), BF),
            pltpu.VMEM((2, ROWS, COLS), F32),
            pltpu.VMEM((2, ROWS, COLS), BF),
            pltpu.VMEM((2, ROWS, 128), F32),
            pltpu.VMEM((2, ROWS, COLS), F32),
            pltpu.VMEM((8, ROWS, COLS), F32),
            pltpu.VMEM((2, 2, ROWS, MID), BF),
            pltpu.VMEM((2, ROWS, MID), BF),
            pltpu.VMEM((2, ROWS, MID), BF),
            pltpu.VMEM((2, 4, ROWS, COLS), BF),
            pltpu.VMEM((2, 4, ROWS, COLS), BF),
            pltpu.VMEM((ROWS, WIDE), BF),
            pltpu.VMEM((ROWS, COLS), BF),
            pltpu.VMEM((32, COLS), F32),
            pltpu.VMEM((2, 4, 4, 64, 128), BF),
            pltpu.VMEM((2, 3, 4, 64, 128), BF),
            pltpu.VMEM((2, 4, 2, 32, 128), BF),
            pltpu.VMEM((2, 7, 32, 128), BF),
            pltpu.VMEM((4, 4, 2, 32, 128), BF),
            pltpu.VMEM((7, 4, 32, 128), BF),
            pltpu.VMEM((4, 32, 128), BF),
            pltpu.VMEM((3, 32, 128), BF),
            pltpu.VMEM((3, 32, 128), BF),
            pltpu.VMEM((3, 7, 32, 128), BF),
            pltpu.VMEM((3, 32, 128), BF),
            pltpu.VMEM((2, 3, 32, 128), BF),
            dma((4,)), dma((3,)),
            *twice(2, 4, 2), *twice(2, 4),
            *twice(3), *twice(4, 3), *twice(4, 4),
            *twice(3), *twice(2, 4, 2),
            *twice(3), *twice(2, 3), *twice(2, 7), *twice(7), *twice(3), *twice(3, 7), *twice(2),
        ],
        compiler_params=pltpu.CompilerParams(
            collective_id=0, has_side_effects=True, vmem_limit_bytes=56 * 2**20
        ),
    )(audio, text, labels, audio_weight)
    return pl.pallas_call(
        hand_over,
        out_shape=shapes,
        in_specs=[pl.BlockSpec(memory_space=pl.ANY)] * 3,
        out_specs=[pl.BlockSpec(memory_space=pl.ANY)] * 3,
        scratch_shapes=[
            pltpu.VMEM((ROWS, WIDE), BF),
            pltpu.VMEM((ROWS, COLS), BF),
            pltpu.VMEM((32, COLS), F32),
            dma((6,)),
        ],
        compiler_params=pltpu.CompilerParams(vmem_limit_bytes=56 * 2**20),
    )(*results)


def solution(mesh):
    rows = P(("blk", "group"), None)
    return jax.shard_map(
        on_device,
        mesh=mesh,
        in_specs=(rows, rows, P(("blk", "group")), P("group", None)),
        out_specs=(rows, rows, P("group", None)),
        check_vma=False,
    )
```

```python
import jax
import jax.numpy as jnp
from jax import lax
from jax.experimental import pallas as pl
from jax.experimental.pallas import tpu as pltpu
from jax.sharding import PartitionSpec as P

MESH = pl.DeviceIdType.MESH
BF = jnp.bfloat16
F32 = jnp.float32
SCALE = 16.0
SHIFT = -4.0
EPS = 1e-6
ROWS, WIDE, COLS, HALF, MID = 160, 1024, 768, 80, 384
AROUND = (1, 7, 2, 6, 3, 5, 4)


def rows_by_columns(a, b):
    return lax.dot_general(a, b, (((1,), (1,)), ((), ())), preferred_element_type=F32)


def kernel(
    audio_hbm, text_hbm, labels_hbm, weight_hbm,
    audio_out, text_out, grad_out,
    labels, audio, audio_t, text, texts, label_rows, label_cols, pair_label, weight, units, unit_low, norms,
    d_audio, d_text, dp_low, dp_other, pair_dp, rs_out, rs_in, audio_res, text_res, grad_res,
    early, gx, gx_in, gz, gz_in, hz, hz_in, hx, hx_in, gy, gy_in, gf, gf_in,
    load_sem, store_sem, gs, gr, ls, lr, w1s, w1r, w2s, w2r, wcs, wcr, ps, pr, rss, rsr,
    cs, cr, xs, xr, zs, zr, hzs, hzr, hxs, hxr, ys, yr, fs, fr,
):
    blk, group = lax.axis_index("blk"), lax.axis_index("group")
    z_lo, y = blk // 8, blk % 8
    z_hi, x, core = group // 8, (group // 2) % 4, group % 2

    def at_y(step):
        return (z_lo * 8 + (y + step + 8) % 8, group)

    def at_x(step):
        return (blk, z_hi * 8 + ((x + step) % 4) * 2 + core)

    def at_z(step):
        there = (z_hi * 2 + z_lo + step + 8) % 8
        return ((there % 2) * 8 + y, (there // 2) * 8 + x * 2 + core)

    pair = ((1 - z_lo) * 8 + y, group)
    other = (blk, z_hi * 8 + x * 2 + (1 - core))
    pair_other = ((1 - z_lo) * 8 + y, z_hi * 8 + x * 2 + (1 - core))
    ring = (at_y(1), at_y(-1))
    started = []

    def send(src, dst, s, r, to):
        copy = pltpu.make_async_remote_copy(
            src_ref=src, dst_ref=dst, send_sem=s, recv_sem=r, device_id=to, device_id_type=MESH
        )
        copy.start()
        started.append(copy)

    def arrived(dst, s, r):
        pltpu.make_async_remote_copy(
            src_ref=dst, dst_ref=dst, send_sem=s, recv_sem=r, device_id=ring[0], device_id_type=MESH
        ).wait_recv()

    barrier = pltpu.get_barrier_semaphore()
    away = 2 * z_lo - 1
    friends = ring + (pair, other, at_z(away), at_z(-2 * away), at_z(3 * away)) + tuple(at_x(i) for i in (1, 2, 3))
    for friend in friends:
        pl.semaphore_signal(barrier, inc=1, device_id=friend, device_id_type=MESH)

    loads = [
        pltpu.make_async_copy(text_hbm, text, load_sem.at[0]),
        pltpu.make_async_copy(weight_hbm, weight.at[z_hi, x * 2 + core], load_sem.at[1]),
        pltpu.make_async_copy(labels_hbm, labels, load_sem.at[3]),
        pltpu.make_async_copy(audio_hbm, audio.at[0], load_sem.at[2]),
    ]
    for load in loads:
        load.start()

    loads[0].wait()
    raw = text[...].astype(F32)
    texts[0] = (raw / jnp.sqrt(jnp.sum(raw * raw, axis=-1, keepdims=True) + EPS)).astype(BF)
    loads[2].wait()
    label_rows[0] = jnp.broadcast_to(labels[...].reshape(1, ROWS).astype(F32), (8, ROWS))
    loads[1].wait()
    loads[3].wait()
    pl.semaphore_wait(barrier, len(friends))

    def part(k):
        return pl.ds(k * HALF, HALF)

    def slot_of(d, hop):
        return 2 * hop - 1 + d if hop < 4 else 7

    def gather_send(d, hop, k):
        src = 0 if hop == 1 else slot_of(d, hop - 1)
        send(
            texts.at[src, part(k)], texts.at[slot_of(d, hop), part(k)],
            gs.at[d, hop - 1, k], gr.at[d, hop - 1, k], ring[d],
        )

    def label_send(d, hop):
        src = 0 if hop == 1 else slot_of(d, hop - 1)
        send(
            label_rows.at[src], label_rows.at[slot_of(d, hop)],
            ls.at[d, hop - 1], lr.at[d, hop - 1], ring[d],
        )

    def gather_hop(hop, turn):
        for d in (0, 1):
            k = d if turn == 0 else 1 - d
            arrived(texts.at[slot_of(d, hop), part(k)], gs.at[d, hop - 1, k], gr.at[d, hop - 1, k])
            if hop < 3 or (hop == 3 and turn == 0):
                gather_send(d, hop + 1, k)

    diagonal = lax.broadcasted_iota(jnp.int32, (ROWS, ROWS), 0) == lax.broadcasted_iota(
        jnp.int32, (ROWS, ROWS), 1
    )

    def label_column(slot):
        row = label_rows[slot][0:1, :]
        column = jnp.sum(jnp.where(diagonal, row, 0.0), axis=1, keepdims=True)
        label_cols[slot] = jnp.broadcast_to(column, (ROWS, 128))

    def label_hop(hop):
        for d in (0, 1):
            if hop == 4 and d == 1:
                continue
            arrived(label_rows.at[slot_of(d, hop)], ls.at[d, hop - 1], lr.at[d, hop - 1])
            if hop < 3 or (hop == 3 and d == 0):
                label_send(d, hop + 1)
            label_column(slot_of(d, hop))

    def near_weight(e, i, side=core):
        return weight.at[(z_hi + 4 + away * (0, 1, -1, 2)[e]) % 4, ((x + 4 - i) % 4) * 2 + side]

    def weight_along_x(e):
        for i in (1, 3, 2):
            send(near_weight(e, 0), near_weight(e, 0), w2s.at[e, i - 1], w2r.at[e, i - 1], at_x(i))
        send(near_weight(e, 0), near_weight(e, 0), wcs.at[e, 0], wcr.at[e, 0], other)

    def weight_from_z(e):
        arrived(near_weight(e, 0), w1s.at[e - 1], w1r.at[e - 1])
        weight_along_x(e)

    def weight_from_x(e):
        for i in (1, 3, 2):
            there = near_weight(e, i)
            arrived(there, w2s.at[e, i - 1], w2r.at[e, i - 1])
            send(there, there, wcs.at[e, i], wcr.at[e, i], other)

    for d in (0, 1):
        gather_send(d, 1, d)
    mine = near_weight(0, 0)
    for e in (3, 2, 1):
        send(mine, mine, w1s.at[e - 1], w1r.at[e - 1], at_z(away * e))
    weight_along_x(0)
    for d in (0, 1):
        gather_send(d, 1, 1 - d)
        label_send(d, 1)
    send(label_rows.at[0], pair_label, ps.at[0], pr.at[0], pair)
    send(audio.at[0], audio.at[1], ps.at[1], pr.at[1], pair)
    send(audio.at[0], audio.at[2], cs.at[0], cr.at[0], other)
    label_column(0)
    audio_t[0] = audio[0].T

    gather_hop(1, 0)
    weight_from_z(1)
    weight_from_z(2)
    gather_hop(1, 1)
    weight_from_z(3)
    label_hop(1)
    weight_from_x(0)
    arrived(audio.at[2], cs.at[0], cr.at[0])
    audio_t[2] = audio[2].T
    gather_hop(2, 0)
    weight_from_x(1)
    weight_from_x(2)
    label_hop(2)
    gather_hop(2, 1)
    arrived(pair_label, ps.at[0], pr.at[0])
    arrived(audio.at[1], ps.at[1], pr.at[1])
    send(audio.at[1], audio.at[3], cs.at[1], cr.at[1], other)
    audio_t[1] = audio[1].T
    def weight_rows(e):
        for i in range(4):
            arrived(near_weight(e, i, 1 - core), wcs.at[e, i], wcr.at[e, i])
        there = (z_hi + 4 + away * (0, 1, -1, 2)[e]) % 4
        for i in (0, 1):
            more = jnp.dot(
                audio[i, :, pl.ds(pl.multiple_of(there * 256, 256), 256)],
                weight[there].reshape(256, COLS),
                preferred_element_type=F32,
            )
            units[i] = more if e == 0 else units[i] + more

    for e in range(3):
        weight_rows(e)
    weight_from_x(3)
    gather_hop(3, 0)
    weight_rows(3)
    for i in (0, 1):
        proj = units[i]
        norm = jnp.sqrt(jnp.sum(proj * proj, axis=-1, keepdims=True) + EPS)
        unit = proj / norm
        units[i] = unit
        norms[i] = jnp.broadcast_to(norm, (ROWS, 128))
        unit_low[i] = unit.astype(BF)

    def blocks(first, count):
        many = count * ROWS
        rows = texts[first : first + count].reshape(many, COLS)
        row_labels = label_cols[first : first + count].reshape(many, 128)[:, 0:1]
        pairs = []
        for i in (0, 1):
            logits = SCALE * rows_by_columns(rows, unit_low[i]) + SHIFT
            own = label_rows[0][0:1, :] if i == 0 else pair_label[0:1, :]
            positive = (row_labels == own).astype(F32)
            pairs.append((SCALE * (jax.nn.sigmoid(logits) - positive)).astype(BF))
        d_text[first : first + count] = (
            jnp.dot(pairs[0], unit_low[0], preferred_element_type=F32)
            + jnp.dot(pairs[1], unit_low[1], preferred_element_type=F32)
        ).reshape(count, ROWS, COLS)
        for i in (0, 1):
            more = lax.dot_general(pairs[i], rows, (((0,), (0,)), ((), ())), preferred_element_type=F32)
            d_audio[i] = more if first == 3 else d_audio[i] + more

    def rs_send(r, turn):
        for d in (0, 1):
            k = d if turn == 0 else 1 - d
            slot = 7 if r == 4 else (2 * r if d == 0 else 2 * r - 1)
            value = d_text[slot, part(k), :]
            if r < 3 or (r == 3 and turn == 0):
                arrived(rs_in.at[d, r, part(k)], rss.at[d, r, k], rsr.at[d, r, k])
                value = value + rs_in[d, r, part(k), :].astype(F32)
            rs_out[d, r - 1, part(k), :] = value.astype(BF)
            send(
                rs_out.at[d, r - 1, part(k)], rs_in.at[d, r - 1, part(k)],
                rss.at[d, r - 1, k], rsr.at[d, r - 1, k], ring[d],
            )

    label_hop(3)
    gather_hop(3, 1)
    blocks(3, 4)
    rs_send(3, 1)
    blocks(0, 3)
    label_hop(4)
    arrived(audio.at[3], cs.at[1], cr.at[1])
    audio_t[3] = audio[3].T
    gather_hop(4, 0)
    blocks(7, 1)
    rs_send(4, 0)

    for i in (1, 0):
        total = d_audio[i]
        unit = units[i]
        share = (total - unit * jnp.sum(unit * total, axis=-1, keepdims=True)) / norms[i][:, 0:1]
        dp_low[0, i] = share[:, :MID].astype(BF)
        dp_low[1, i] = share[:, MID:].astype(BF)
        if i == 0:
            d_audio[0] = share
        send(dp_low.at[1 - core, i], dp_other.at[i], cs.at[2 + i], cr.at[2 + i], other)

    def of_core(cut):
        total = jnp.dot(audio_t[0], dp_low[core, 0, :, cut], preferred_element_type=F32)
        return total + jnp.dot(audio_t[1], dp_low[core, 1, :, cut], preferred_element_type=F32)

    early[...] = of_core(pl.ds(0, 256))
    for i in (1, 0):
        arrived(dp_other.at[i], cs.at[2 + i], cr.at[2 + i])

    def product(cut, total):
        total += jnp.dot(audio_t[2], dp_other[0, :, cut], preferred_element_type=F32)
        return total + jnp.dot(audio_t[3], dp_other[1, :, cut], preferred_element_type=F32)

    first = product(pl.ds(0, 256), early[...]).astype(BF)
    for j in (0, 1):
        gx[j] = first[:, j * 128 : j * 128 + 128].reshape(4, 4, 64, 128)
        for i in (2, 1, 3):
            send(gx.at[j, :, (x + i) % 4], gx_in.at[j, i - 1], xs.at[j, i - 1], xr.at[j, i - 1], at_x(i))
    hz[...] = product(pl.ds(256, 128), of_core(pl.ds(256, 128))).astype(BF).reshape(4, 4, 2, 32, 128)
    for i in AROUND:
        there = (z_hi * 2 + z_lo + i) % 8
        send(hz.at[there // 2, :, there % 2], hz_in.at[i - 1], hzs.at[i - 1], hzr.at[i - 1], at_z(i))

    def along_z(j):
        total = gx[j, :, x].astype(F32)
        for i in (1, 3, 2):
            arrived(gx_in.at[j, i - 1], xs.at[j, i - 1], xr.at[j, i - 1])
            total += gx_in[j, i - 1].astype(F32)
        gz[j] = total.astype(BF).reshape(4, 2, 32, 128)
        for i in AROUND:
            there = (z_hi * 2 + z_lo + i) % 8
            send(gz.at[j, there // 2, there % 2], gz_in.at[j, i - 1], zs.at[j, i - 1], zr.at[j, i - 1], at_z(i))

    def along_x():
        total = hz[z_hi, :, z_lo].astype(F32)
        for i in AROUND:
            arrived(hz_in.at[i - 1], hzs.at[i - 1], hzr.at[i - 1])
            total += hz_in[i - 1].astype(F32)
        hx[...] = total.astype(BF)
        for i in (2, 1, 3):
            send(hx.at[(x + i) % 4], hx_in.at[i - 1], hxs.at[i - 1], hxr.at[i - 1], at_x(i))

    def along_y(j):
        if j < 2:
            total = gz[j, z_hi, z_lo].astype(F32)
            for i in AROUND:
                arrived(gz_in.at[j, i - 1], zs.at[j, i - 1], zr.at[j, i - 1])
                total += gz_in[j, i - 1].astype(F32)
        else:
            total = hx[x].astype(F32)
            for i in (1, 3, 2):
                arrived(hx_in.at[i - 1], hxs.at[i - 1], hxr.at[i - 1])
                total += hx_in[i - 1].astype(F32)
        gy[j] = total.astype(BF)
        for i in AROUND:
            send(gy.at[j], gy_in.at[j, i - 1], ys.at[j, i - 1], yr.at[j, i - 1], at_y(i))

    def complete(j):
        total = gy[j].astype(F32)
        for i in AROUND:
            arrived(gy_in.at[j, i - 1], ys.at[j, i - 1], yr.at[j, i - 1])
            total += gy_in[j, i - 1].astype(F32)
        gf[j] = total.astype(BF)

    rs_send(2, 1)
    rs_send(3, 0)
    along_z(0)
    along_z(1)
    send(dp_low.at[:, 1], pair_dp, ps.at[2], pr.at[2], pair)
    rs_send(1, 1)
    rs_send(2, 0)
    along_x()
    along_y(0)
    along_y(2)
    along_y(1)
    rs_send(1, 0)

    complete(0)
    complete(2)
    complete(1)

    def final(to, k):
        return pltpu.make_async_remote_copy(
            src_ref=gf, dst_ref=gf_in.at[core], send_sem=fs.at[k], recv_sem=fr.at[core],
            device_id=to, device_id_type=MESH,
        )

    def landed(half):
        arrived(gf_in.at[half], fs.at[0], fr.at[half])

    @pl.when(core == z_lo)
    def _():
        final(pair, 0).start()
        gf_in[core] = gf[...]

    @pl.when(core != z_lo)
    def _():
        final(pair_other, 0).start()
        final(other, 1).start()

    arrived(pair_dp, ps.at[2], pr.at[2])
    both = jnp.concatenate([pair_dp[0], pair_dp[1]], axis=1).astype(F32)
    dproj = (d_audio[0] + both).astype(BF)
    audio_res[...] = rows_by_columns(dproj, weight[...].reshape(WIDE, COLS)).astype(BF)
    store_audio = pltpu.make_async_copy(audio_res, audio_out, store_sem.at[0])
    store_audio.start()

    for turn in (1, 0):
        for k in (0, 1):
            d = k if turn == 0 else 1 - k
            arrived(rs_in.at[d, 0, part(k)], rss.at[d, 0, k], rsr.at[d, 0, k])
    raw = text[...].astype(F32)
    norm = jnp.sqrt(jnp.sum(raw * raw, axis=-1, keepdims=True) + EPS)
    unit = raw / norm
    total = d_text[0] + rs_in[0, 0].astype(F32) + rs_in[1, 0].astype(F32)
    text_res[...] = ((total - unit * jnp.sum(unit * total, axis=-1, keepdims=True)) / norm).astype(BF)
    store_text = pltpu.make_async_copy(text_res, text_out, store_sem.at[1])
    store_text.start()

    @pl.when(core == z_lo)
    def _():
        landed(1 - core)
        final(pair, 0).wait_send()

    @pl.when(core != z_lo)
    def _():
        landed(0)
        landed(1)
        final(pair_other, 0).wait_send()
        final(other, 1).wait_send()

    for half in (0, 1):
        for j in range(3):
            grad_res[:, pl.ds(half * MID + j * 128, 128)] = gf_in[half, j].astype(F32)
    store_grad = pltpu.make_async_copy(grad_res, grad_out, store_sem.at[2])
    store_grad.start()
    for copy in started:
        copy.wait_send()
    store_audio.wait()
    store_text.wait()
    store_grad.wait()


def hand_over(audio_in, text_in, grad_in, audio_out, text_out, grad_out, audio, text, grad, sems):
    ways = ((audio_in, audio, audio_out), (text_in, text, text_out), (grad_in, grad, grad_out))
    loads = [pltpu.make_async_copy(src, by, sems.at[i]) for i, (src, by, _) in enumerate(ways)]
    stores = [pltpu.make_async_copy(by, dst, sems.at[3 + i]) for i, (_, by, dst) in enumerate(ways)]
    for load in loads:
        load.start()
    for load, store in zip(loads, stores):
        load.wait()
        store.start()
    for store in stores:
        store.wait()


def on_device(audio, text, labels, audio_weight):
    dma = pltpu.SemaphoreType.DMA
    twice = lambda *shape: [dma(shape), dma(shape)]
    shapes = (
        jax.ShapeDtypeStruct((ROWS, WIDE), BF),
        jax.ShapeDtypeStruct((ROWS, COLS), BF),
        jax.ShapeDtypeStruct((32, COLS), F32),
    )
    results = pl.pallas_call(
        kernel,
        out_shape=shapes,
        in_specs=[pl.BlockSpec(memory_space=pltpu.HBM)] * 4,
        out_specs=[pl.BlockSpec(memory_space=pltpu.HBM)] * 3,
        scratch_shapes=[
            pltpu.VMEM((ROWS,), jnp.int32),
            pltpu.VMEM((4, ROWS, WIDE), BF),
            pltpu.VMEM((4, WIDE, ROWS), BF),
            pltpu.VMEM((ROWS, COLS), BF),
            pltpu.VMEM((8, ROWS, COLS), BF),
            pltpu.VMEM((8, 8, ROWS), F32),
            pltpu.VMEM((8, ROWS, 128), F32),
            pltpu.VMEM((8, ROWS), F32),
            pltpu.VMEM((4, 8, 32, COLS), BF),
            pltpu.VMEM((2, ROWS, COLS), F32),
            pltpu.VMEM((2, ROWS, COLS), BF),
            pltpu.VMEM((2, ROWS, 128), F32),
            pltpu.VMEM((2, ROWS, COLS), F32),
            pltpu.VMEM((8, ROWS, COLS), F32),
            pltpu.VMEM((2, 2, ROWS, MID), BF),
            pltpu.VMEM((2, ROWS, MID), BF),
            pltpu.VMEM((2, ROWS, MID), BF),
            pltpu.VMEM((2, 4, ROWS, COLS), BF),
            pltpu.VMEM((2, 4, ROWS, COLS), BF),
            pltpu.VMEM((ROWS, WIDE), BF),
            pltpu.VMEM((ROWS, COLS), BF),
            pltpu.VMEM((32, COLS), F32),
            pltpu.VMEM((WIDE, 256), F32),
            pltpu.VMEM((2, 4, 4, 64, 128), BF),
            pltpu.VMEM((2, 3, 4, 64, 128), BF),
            pltpu.VMEM((2, 4, 2, 32, 128), BF),
            pltpu.VMEM((2, 7, 32, 128), BF),
            pltpu.VMEM((4, 4, 2, 32, 128), BF),
            pltpu.VMEM((7, 4, 32, 128), BF),
            pltpu.VMEM((4, 32, 128), BF),
            pltpu.VMEM((3, 32, 128), BF),
            pltpu.VMEM((3, 32, 128), BF),
            pltpu.VMEM((3, 7, 32, 128), BF),
            pltpu.VMEM((3, 32, 128), BF),
            pltpu.VMEM((2, 3, 32, 128), BF),
            dma((4,)), dma((3,)),
            *twice(2, 4, 2), *twice(2, 4),
            *twice(3), *twice(4, 3), *twice(4, 4),
            *twice(3), *twice(2, 4, 2),
            *twice(4), *twice(2, 3), *twice(2, 7), *twice(7), *twice(3), *twice(3, 7), *twice(2),
        ],
        compiler_params=pltpu.CompilerParams(
            collective_id=0, has_side_effects=True, vmem_limit_bytes=56 * 2**20
        ),
    )(audio, text, labels, audio_weight)
    return pl.pallas_call(
        hand_over,
        out_shape=shapes,
        in_specs=[pl.BlockSpec(memory_space=pl.ANY)] * 3,
        out_specs=[pl.BlockSpec(memory_space=pl.ANY)] * 3,
        scratch_shapes=[
            pltpu.VMEM((ROWS, WIDE), BF),
            pltpu.VMEM((ROWS, COLS), BF),
            pltpu.VMEM((32, COLS), F32),
            dma((6,)),
        ],
        compiler_params=pltpu.CompilerParams(vmem_limit_bytes=56 * 2**20),
    )(*results)


def solution(mesh):
    rows = P(("blk", "group"), None)
    return jax.shard_map(
        on_device,
        mesh=mesh,
        in_specs=(rows, rows, P(("blk", "group")), P("group", None)),
        out_specs=(rows, rows, P("group", None)),
        check_vma=False,
    )
```

```python
import jax
import jax.numpy as jnp
from jax import lax
from jax.experimental import pallas as pl
from jax.experimental.pallas import tpu as pltpu
from jax.sharding import PartitionSpec as P

MESH = pl.DeviceIdType.MESH
BF = jnp.bfloat16
F32 = jnp.float32
SCALE = 16.0
SHIFT = -4.0
EPS = 1e-6
ROWS, WIDE, COLS, HALF, MID = 160, 1024, 768, 80, 384
AROUND = (4, 3, 5, 2, 6, 1, 7)


def rows_by_columns(a, b):
    return lax.dot_general(a, b, (((1,), (1,)), ((), ())), preferred_element_type=F32)


def kernel(
    audio_hbm, text_hbm, labels_hbm, weight_hbm,
    audio_out, text_out, grad_out,
    labels, audio, audio_t, text, texts, label_rows, label_cols, pair_label, weight, units, unit_low, norms,
    d_audio, d_text, dp_low, dp_other, pair_dp, rs_out, rs_in, audio_res, text_res, grad_res,
    early, gx, gx_in, gz, gz_in, hz, hz_in, hx, hx_in, gy, gy_in, gf, gf_in,
    load_sem, store_sem, gs, gr, ls, lr, w1s, w1r, w2s, w2r, wcs, wcr, ps, pr, rss, rsr,
    cs, cr, xs, xr, zs, zr, hzs, hzr, hxs, hxr, ys, yr, fs, fr,
):
    blk, group = lax.axis_index("blk"), lax.axis_index("group")
    z_lo, y = blk // 8, blk % 8
    z_hi, x, core = group // 8, (group // 2) % 4, group % 2

    def at_y(step):
        return (z_lo * 8 + (y + step + 8) % 8, group)

    def at_x(step):
        return (blk, z_hi * 8 + ((x + step) % 4) * 2 + core)

    def at_z(step):
        there = (z_hi * 2 + z_lo + step + 8) % 8
        return ((there % 2) * 8 + y, (there // 2) * 8 + x * 2 + core)

    pair = ((1 - z_lo) * 8 + y, group)
    other = (blk, z_hi * 8 + x * 2 + (1 - core))
    pair_other = ((1 - z_lo) * 8 + y, z_hi * 8 + x * 2 + (1 - core))
    ring = (at_y(1), at_y(-1))
    started = []

    def send(src, dst, s, r, to):
        copy = pltpu.make_async_remote_copy(
            src_ref=src, dst_ref=dst, send_sem=s, recv_sem=r, device_id=to, device_id_type=MESH
        )
        copy.start()
        started.append(copy)

    def arrived(dst, s, r):
        pltpu.make_async_remote_copy(
            src_ref=dst, dst_ref=dst, send_sem=s, recv_sem=r, device_id=ring[0], device_id_type=MESH
        ).wait_recv()

    barrier = pltpu.get_barrier_semaphore()
    away = 2 * z_lo - 1
    friends = ring + (pair, other, at_z(away), at_z(-2 * away), at_z(3 * away)) + tuple(at_x(i) for i in (1, 2, 3))
    for friend in friends:
        pl.semaphore_signal(barrier, inc=1, device_id=friend, device_id_type=MESH)

    loads = [
        pltpu.make_async_copy(text_hbm, text, load_sem.at[0]),
        pltpu.make_async_copy(weight_hbm, weight.at[z_hi, x * 2 + core], load_sem.at[1]),
        pltpu.make_async_copy(labels_hbm, labels, load_sem.at[3]),
        pltpu.make_async_copy(audio_hbm, audio.at[0], load_sem.at[2]),
    ]
    for load in loads:
        load.start()

    loads[0].wait()
    raw = text[...].astype(F32)
    texts[0] = (raw / jnp.sqrt(jnp.sum(raw * raw, axis=-1, keepdims=True) + EPS)).astype(BF)
    loads[2].wait()
    label_rows[0] = jnp.broadcast_to(labels[...].reshape(1, ROWS).astype(F32), (8, ROWS))
    loads[1].wait()
    loads[3].wait()
    pl.semaphore_wait(barrier, len(friends))

    def part(k):
        return pl.ds(k * HALF, HALF)

    def slot_of(d, hop):
        return 2 * hop - 1 + d if hop < 4 else 7

    def gather_send(d, hop, k):
        src = 0 if hop == 1 else slot_of(d, hop - 1)
        send(
            texts.at[src, part(k)], texts.at[slot_of(d, hop), part(k)],
            gs.at[d, hop - 1, k], gr.at[d, hop - 1, k], ring[d],
        )

    def label_send(d, hop):
        src = 0 if hop == 1 else slot_of(d, hop - 1)
        send(
            label_rows.at[src], label_rows.at[slot_of(d, hop)],
            ls.at[d, hop - 1], lr.at[d, hop - 1], ring[d],
        )

    def gather_hop(hop, turn):
        for d in (0, 1):
            k = d if turn == 0 else 1 - d
            arrived(texts.at[slot_of(d, hop), part(k)], gs.at[d, hop - 1, k], gr.at[d, hop - 1, k])
            if hop < 3 or (hop == 3 and turn == 0):
                gather_send(d, hop + 1, k)

    diagonal = lax.broadcasted_iota(jnp.int32, (ROWS, ROWS), 0) == lax.broadcasted_iota(
        jnp.int32, (ROWS, ROWS), 1
    )

    def label_column(slot):
        row = label_rows[slot][0:1, :]
        column = jnp.sum(jnp.where(diagonal, row, 0.0), axis=1, keepdims=True)
        label_cols[slot] = jnp.broadcast_to(column, (ROWS, 128))

    def label_hop(hop):
        for d in (0, 1):
            if hop == 4 and d == 1:
                continue
            arrived(label_rows.at[slot_of(d, hop)], ls.at[d, hop - 1], lr.at[d, hop - 1])
            if hop < 3 or (hop == 3 and d == 0):
                label_send(d, hop + 1)
            label_column(slot_of(d, hop))

    def near_weight(e, i, side=core):
        return weight.at[(z_hi + 4 + away * (0, 1, -1, 2)[e]) % 4, ((x + 4 - i) % 4) * 2 + side]

    def weight_along_x(e):
        for i in (1, 3, 2):
            send(near_weight(e, 0), near_weight(e, 0), w2s.at[e, i - 1], w2r.at[e, i - 1], at_x(i))
        send(near_weight(e, 0), near_weight(e, 0), wcs.at[e, 0], wcr.at[e, 0], other)

    def weight_from_z(e):
        arrived(near_weight(e, 0), w1s.at[e - 1], w1r.at[e - 1])
        weight_along_x(e)

    def weight_from_x(e):
        for i in (1, 3, 2):
            there = near_weight(e, i)
            arrived(there, w2s.at[e, i - 1], w2r.at[e, i - 1])
            send(there, there, wcs.at[e, i], wcr.at[e, i], other)

    for d in (0, 1):
        gather_send(d, 1, d)
    mine = near_weight(0, 0)
    for e in (3, 2, 1):
        send(mine, mine, w1s.at[e - 1], w1r.at[e - 1], at_z(away * e))
    weight_along_x(0)
    for d in (0, 1):
        gather_send(d, 1, 1 - d)
        label_send(d, 1)
    send(label_rows.at[0], pair_label, ps.at[0], pr.at[0], pair)
    send(audio.at[0], audio.at[1], ps.at[1], pr.at[1], pair)
    send(audio.at[0], audio.at[2], cs.at[0], cr.at[0], other)
    label_column(0)
    audio_t[0] = audio[0].T

    gather_hop(1, 0)
    weight_from_z(1)
    weight_from_z(2)
    gather_hop(1, 1)
    weight_from_z(3)
    label_hop(1)
    weight_from_x(0)
    arrived(audio.at[2], cs.at[0], cr.at[0])
    audio_t[2] = audio[2].T
    gather_hop(2, 0)
    weight_from_x(1)
    weight_from_x(2)
    label_hop(2)
    gather_hop(2, 1)
    arrived(pair_label, ps.at[0], pr.at[0])
    arrived(audio.at[1], ps.at[1], pr.at[1])
    send(audio.at[1], audio.at[3], cs.at[1], cr.at[1], other)
    audio_t[1] = audio[1].T
    def weight_rows(e):
        for i in range(4):
            arrived(near_weight(e, i, 1 - core), wcs.at[e, i], wcr.at[e, i])
        there = (z_hi + 4 + away * (0, 1, -1, 2)[e]) % 4
        for i in (0, 1):
            more = jnp.dot(
                audio[i, :, pl.ds(pl.multiple_of(there * 256, 256), 256)],
                weight[there].reshape(256, COLS),
                preferred_element_type=F32,
            )
            units[i] = more if e == 0 else units[i] + more

    for e in range(3):
        weight_rows(e)
    weight_from_x(3)
    gather_hop(3, 0)
    weight_rows(3)
    for i in (0, 1):
        proj = units[i]
        norm = jnp.sqrt(jnp.sum(proj * proj, axis=-1, keepdims=True) + EPS)
        unit = proj / norm
        units[i] = unit
        norms[i] = jnp.broadcast_to(norm, (ROWS, 128))
        unit_low[i] = unit.astype(BF)

    def blocks(first, count):
        many = count * ROWS
        rows = texts[first : first + count].reshape(many, COLS)
        row_labels = label_cols[first : first + count].reshape(many, 128)[:, 0:1]
        pairs = []
        for i in (0, 1):
            logits = SCALE * rows_by_columns(rows, unit_low[i]) + SHIFT
            own = label_rows[0][0:1, :] if i == 0 else pair_label[0:1, :]
            positive = (row_labels == own).astype(F32)
            pairs.append((SCALE * (jax.nn.sigmoid(logits) - positive)).astype(BF))
        d_text[first : first + count] = (
            jnp.dot(pairs[0], unit_low[0], preferred_element_type=F32)
            + jnp.dot(pairs[1], unit_low[1], preferred_element_type=F32)
        ).reshape(count, ROWS, COLS)
        for i in (0, 1):
            more = lax.dot_general(pairs[i], rows, (((0,), (0,)), ((), ())), preferred_element_type=F32)
            d_audio[i] = more if first == 3 else d_audio[i] + more

    def rs_send(r, turn):
        for d in (0, 1):
            k = d if turn == 0 else 1 - d
            slot = 7 if r == 4 else (2 * r if d == 0 else 2 * r - 1)
            value = d_text[slot, part(k), :]
            if r < 3 or (r == 3 and turn == 0):
                arrived(rs_in.at[d, r, part(k)], rss.at[d, r, k], rsr.at[d, r, k])
                value = value + rs_in[d, r, part(k), :].astype(F32)
            rs_out[d, r - 1, part(k), :] = value.astype(BF)
            send(
                rs_out.at[d, r - 1, part(k)], rs_in.at[d, r - 1, part(k)],
                rss.at[d, r - 1, k], rsr.at[d, r - 1, k], ring[d],
            )

    label_hop(3)
    gather_hop(3, 1)
    blocks(3, 4)
    rs_send(3, 1)
    blocks(0, 3)
    label_hop(4)
    arrived(audio.at[3], cs.at[1], cr.at[1])
    audio_t[3] = audio[3].T
    gather_hop(4, 0)
    blocks(7, 1)
    rs_send(4, 0)

    for i in (1, 0):
        total = d_audio[i]
        unit = units[i]
        share = (total - unit * jnp.sum(unit * total, axis=-1, keepdims=True)) / norms[i][:, 0:1]
        dp_low[0, i] = share[:, :MID].astype(BF)
        dp_low[1, i] = share[:, MID:].astype(BF)
        if i == 0:
            d_audio[0] = share
        send(dp_low.at[1 - core, i], dp_other.at[i], cs.at[2 + i], cr.at[2 + i], other)

    def of_core(cut):
        total = jnp.dot(audio_t[0], dp_low[core, 0, :, cut], preferred_element_type=F32)
        return total + jnp.dot(audio_t[1], dp_low[core, 1, :, cut], preferred_element_type=F32)

    early[...] = of_core(pl.ds(0, 256))
    for i in (1, 0):
        arrived(dp_other.at[i], cs.at[2 + i], cr.at[2 + i])

    def product(cut, total):
        total += jnp.dot(audio_t[2], dp_other[0, :, cut], preferred_element_type=F32)
        return total + jnp.dot(audio_t[3], dp_other[1, :, cut], preferred_element_type=F32)

    first = product(pl.ds(0, 256), early[...]).astype(BF)
    for j in (0, 1):
        gx[j] = first[:, j * 128 : j * 128 + 128].reshape(4, 4, 64, 128)
        for i in (2, 1, 3):
            send(gx.at[j, :, (x + i) % 4], gx_in.at[j, i - 1], xs.at[j, i - 1], xr.at[j, i - 1], at_x(i))
    hz[...] = product(pl.ds(256, 128), of_core(pl.ds(256, 128))).astype(BF).reshape(4, 4, 2, 32, 128)
    for i in AROUND:
        there = (z_hi * 2 + z_lo + i) % 8
        send(hz.at[there // 2, :, there % 2], hz_in.at[i - 1], hzs.at[i - 1], hzr.at[i - 1], at_z(i))

    def along_z(j):
        total = gx[j, :, x].astype(F32)
        for i in (1, 3, 2):
            arrived(gx_in.at[j, i - 1], xs.at[j, i - 1], xr.at[j, i - 1])
            total += gx_in[j, i - 1].astype(F32)
        gz[j] = total.astype(BF).reshape(4, 2, 32, 128)
        for i in AROUND:
            there = (z_hi * 2 + z_lo + i) % 8
            send(gz.at[j, there // 2, there % 2], gz_in.at[j, i - 1], zs.at[j, i - 1], zr.at[j, i - 1], at_z(i))

    def along_x():
        total = hz[z_hi, :, z_lo].astype(F32)
        for i in AROUND:
            arrived(hz_in.at[i - 1], hzs.at[i - 1], hzr.at[i - 1])
            total += hz_in[i - 1].astype(F32)
        hx[...] = total.astype(BF)
        for i in (2, 1, 3):
            send(hx.at[(x + i) % 4], hx_in.at[i - 1], hxs.at[i - 1], hxr.at[i - 1], at_x(i))

    def along_y(j):
        if j < 2:
            total = gz[j, z_hi, z_lo].astype(F32)
            for i in AROUND:
                arrived(gz_in.at[j, i - 1], zs.at[j, i - 1], zr.at[j, i - 1])
                total += gz_in[j, i - 1].astype(F32)
        else:
            total = hx[x].astype(F32)
            for i in (1, 3, 2):
                arrived(hx_in.at[i - 1], hxs.at[i - 1], hxr.at[i - 1])
                total += hx_in[i - 1].astype(F32)
        gy[j] = total.astype(BF)
        for i in AROUND:
            send(gy.at[j], gy_in.at[j, i - 1], ys.at[j, i - 1], yr.at[j, i - 1], at_y(i))

    def complete(j):
        total = gy[j].astype(F32)
        for i in AROUND:
            arrived(gy_in.at[j, i - 1], ys.at[j, i - 1], yr.at[j, i - 1])
            total += gy_in[j, i - 1].astype(F32)
        gf[j] = total.astype(BF)

    rs_send(2, 1)
    rs_send(3, 0)
    along_z(0)
    along_z(1)
    send(dp_low.at[:, 1], pair_dp, ps.at[2], pr.at[2], pair)
    rs_send(1, 1)
    rs_send(2, 0)
    along_x()
    along_y(0)
    along_y(1)
    along_y(2)
    rs_send(1, 0)

    complete(0)
    complete(1)
    complete(2)

    def final(to, k):
        return pltpu.make_async_remote_copy(
            src_ref=gf, dst_ref=gf_in.at[core], send_sem=fs.at[k], recv_sem=fr.at[core],
            device_id=to, device_id_type=MESH,
        )

    def landed(half):
        arrived(gf_in.at[half], fs.at[0], fr.at[half])

    @pl.when(core == z_lo)
    def _():
        final(pair, 0).start()
        gf_in[core] = gf[...]

    @pl.when(core != z_lo)
    def _():
        final(pair_other, 0).start()
        final(other, 1).start()

    arrived(pair_dp, ps.at[2], pr.at[2])
    both = jnp.concatenate([pair_dp[0], pair_dp[1]], axis=1).astype(F32)
    dproj = (d_audio[0] + both).astype(BF)
    audio_res[...] = rows_by_columns(dproj, weight[...].reshape(WIDE, COLS)).astype(BF)
    store_audio = pltpu.make_async_copy(audio_res, audio_out, store_sem.at[0])
    store_audio.start()

    for turn in (1, 0):
        for k in (0, 1):
            d = k if turn == 0 else 1 - k
            arrived(rs_in.at[d, 0, part(k)], rss.at[d, 0, k], rsr.at[d, 0, k])
    raw = text[...].astype(F32)
    norm = jnp.sqrt(jnp.sum(raw * raw, axis=-1, keepdims=True) + EPS)
    unit = raw / norm
    total = d_text[0] + rs_in[0, 0].astype(F32) + rs_in[1, 0].astype(F32)
    text_res[...] = ((total - unit * jnp.sum(unit * total, axis=-1, keepdims=True)) / norm).astype(BF)
    store_text = pltpu.make_async_copy(text_res, text_out, store_sem.at[1])
    store_text.start()

    @pl.when(core == z_lo)
    def _():
        landed(1 - core)
        final(pair, 0).wait_send()

    @pl.when(core != z_lo)
    def _():
        landed(0)
        landed(1)
        final(pair_other, 0).wait_send()
        final(other, 1).wait_send()

    for half in (0, 1):
        for j in range(3):
            grad_res[:, pl.ds(half * MID + j * 128, 128)] = gf_in[half, j].astype(F32)
    store_grad = pltpu.make_async_copy(grad_res, grad_out, store_sem.at[2])
    store_grad.start()
    for copy in started:
        copy.wait_send()
    store_audio.wait()
    store_text.wait()
    store_grad.wait()


def hand_over(audio_in, text_in, grad_in, audio_out, text_out, grad_out, audio, text, grad, sems):
    ways = ((audio_in, audio, audio_out), (text_in, text, text_out), (grad_in, grad, grad_out))
    loads = [pltpu.make_async_copy(src, by, sems.at[i]) for i, (src, by, _) in enumerate(ways)]
    stores = [pltpu.make_async_copy(by, dst, sems.at[3 + i]) for i, (_, by, dst) in enumerate(ways)]
    for load in loads:
        load.start()
    for load, store in zip(loads, stores):
        load.wait()
        store.start()
    for store in stores:
        store.wait()


def on_device(audio, text, labels, audio_weight):
    dma = pltpu.SemaphoreType.DMA
    twice = lambda *shape: [dma(shape), dma(shape)]
    shapes = (
        jax.ShapeDtypeStruct((ROWS, WIDE), BF),
        jax.ShapeDtypeStruct((ROWS, COLS), BF),
        jax.ShapeDtypeStruct((32, COLS), F32),
    )
    results = pl.pallas_call(
        kernel,
        out_shape=shapes,
        in_specs=[pl.BlockSpec(memory_space=pltpu.HBM)] * 4,
        out_specs=[pl.BlockSpec(memory_space=pltpu.HBM)] * 3,
        scratch_shapes=[
            pltpu.VMEM((ROWS,), jnp.int32),
            pltpu.VMEM((4, ROWS, WIDE), BF),
            pltpu.VMEM((4, WIDE, ROWS), BF),
            pltpu.VMEM((ROWS, COLS), BF),
            pltpu.VMEM((8, ROWS, COLS), BF),
            pltpu.VMEM((8, 8, ROWS), F32),
            pltpu.VMEM((8, ROWS, 128), F32),
            pltpu.VMEM((8, ROWS), F32),
            pltpu.VMEM((4, 8, 32, COLS), BF),
            pltpu.VMEM((2, ROWS, COLS), F32),
            pltpu.VMEM((2, ROWS, COLS), BF),
            pltpu.VMEM((2, ROWS, 128), F32),
            pltpu.VMEM((2, ROWS, COLS), F32),
            pltpu.VMEM((8, ROWS, COLS), F32),
            pltpu.VMEM((2, 2, ROWS, MID), BF),
            pltpu.VMEM((2, ROWS, MID), BF),
            pltpu.VMEM((2, ROWS, MID), BF),
            pltpu.VMEM((2, 4, ROWS, COLS), BF),
            pltpu.VMEM((2, 4, ROWS, COLS), BF),
            pltpu.VMEM((ROWS, WIDE), BF),
            pltpu.VMEM((ROWS, COLS), BF),
            pltpu.VMEM((32, COLS), F32),
            pltpu.VMEM((WIDE, 256), F32),
            pltpu.VMEM((2, 4, 4, 64, 128), BF),
            pltpu.VMEM((2, 3, 4, 64, 128), BF),
            pltpu.VMEM((2, 4, 2, 32, 128), BF),
            pltpu.VMEM((2, 7, 32, 128), BF),
            pltpu.VMEM((4, 4, 2, 32, 128), BF),
            pltpu.VMEM((7, 4, 32, 128), BF),
            pltpu.VMEM((4, 32, 128), BF),
            pltpu.VMEM((3, 32, 128), BF),
            pltpu.VMEM((3, 32, 128), BF),
            pltpu.VMEM((3, 7, 32, 128), BF),
            pltpu.VMEM((3, 32, 128), BF),
            pltpu.VMEM((2, 3, 32, 128), BF),
            dma((4,)), dma((3,)),
            *twice(2, 4, 2), *twice(2, 4),
            *twice(3), *twice(4, 3), *twice(4, 4),
            *twice(3), *twice(2, 4, 2),
            *twice(4), *twice(2, 3), *twice(2, 7), *twice(7), *twice(3), *twice(3, 7), *twice(2),
        ],
        compiler_params=pltpu.CompilerParams(
            collective_id=0, has_side_effects=True, vmem_limit_bytes=56 * 2**20
        ),
    )(audio, text, labels, audio_weight)
    return pl.pallas_call(
        hand_over,
        out_shape=shapes,
        in_specs=[pl.BlockSpec(memory_space=pl.ANY)] * 3,
        out_specs=[pl.BlockSpec(memory_space=pl.ANY)] * 3,
        scratch_shapes=[
            pltpu.VMEM((ROWS, WIDE), BF),
            pltpu.VMEM((ROWS, COLS), BF),
            pltpu.VMEM((32, COLS), F32),
            dma((6,)),
        ],
        compiler_params=pltpu.CompilerParams(vmem_limit_bytes=56 * 2**20),
    )(*results)


def solution(mesh):
    rows = P(("blk", "group"), None)
    return jax.shard_map(
        on_device,
        mesh=mesh,
        in_specs=(rows, rows, P(("blk", "group")), P("group", None)),
        out_specs=(rows, rows, P("group", None)),
        check_vma=False,
    )
```
